768 devices in a mesh: row: 24 (over z_hi, y), col: 32 (over z_lo, x, core).
Axes of the slice: x: 4, y: 8, z: 12 (z_hi: 3, z_lo: 4; z = z_hi * 4 + z_lo), core: 2. Of those that a mesh axis runs over, the one named last changes fastest.
Arguments:
- iterate_tiles: bfloat16 [3072, 12288], P('row', 'col'), may hold values from -1.5 to 1.5
- tile_blocks: int32 [48, 96], P('row', 'col'), may hold values from -1 to 383, as said below
Outputs:
- next_tiles: bfloat16 [3072, 12288], P('row', 'col')
The draws below stay inside these ranges and needn't reach their ends.
Inputs may be any that keep to these rules, and one draw needn't show every extreme that they name: `tile_blocks`: A used slot on process row p and process column q holds a block (I, J) with I mod (number of process rows) = p and (J + (J div number of process rows)) mod (number of process columns) = q, so a block's process column depends on its block column alone. No block appears twice, every diagonal block (I, I) appears, and unused slots hold -1 in both rows. At least one device uses all 3 slots; the order of slots within a device carries no meaning.
All inputs are finite; a program needn't handle non-finite values.
Results may differ from the reference program's by a relative error of at most 0.0048.
Values may be sent and summed in bfloat16 or wider, within the bound.
No kernel may reach another device: no remote copies, remote signals or barrier semaphores. Data moves between devices by JAX's collectives and lax.ppermute only.
A program may use at most 32 MiB of HBM per device.

```python
import jax
import jax.numpy as jnp
from jax import lax

BLK = 128
NB = 384
EXTRA_DEV = 2
DIAG_DEV = 1
CAP = 3
N_ROW = 24
N_COL = 32


def draw_tile_blocks(key, part):
    key = jax.random.fold_in(key, 11)
    cell_key, count_key, chosen_key, order_key = jax.random.split(key, 4)
    rows_dev = NB // N_ROW
    shape_dev = (N_ROW, N_COL, rows_dev)
    row_ids = jnp.arange(N_ROW, dtype=jnp.int32)[:, None, None]
    col_ids = jnp.arange(N_COL, dtype=jnp.int32)[None, :, None]
    step_ids = jnp.arange(rows_dev, dtype=jnp.int32)[None, None, :]
    diag_block = jnp.broadcast_to(row_ids + N_ROW * step_ids, shape_dev)
    diag_owned = jnp.broadcast_to((row_ids + (N_ROW + 1) * step_ids) % N_COL == col_ids, shape_dev)
    diag_rank = jnp.where(diag_owned, 0, rows_dev) + step_ids
    diag_pick = jnp.argsort(diag_rank, axis=-1)[..., :DIAG_DEV].astype(jnp.int32)
    diag_rows = jnp.take_along_axis(diag_block, diag_pick, axis=-1)
    diag_live = jnp.take_along_axis(diag_owned, diag_pick, axis=-1)
    cell_total = rows_dev * NB
    cell_ids = jnp.arange(cell_total, dtype=jnp.int32)[None, None, :]
    cell_col = cell_ids % NB
    cell_row = row_ids + N_ROW * (cell_ids // NB)
    col_owner = (cell_col + cell_col // N_ROW) % N_COL
    allowed = (col_owner == col_ids) & (cell_col != cell_row)
    noise_draw = jax.random.randint(cell_key, (N_ROW, N_COL, cell_total), 0, 1024, dtype=jnp.int32)
    cell_score = jnp.where(allowed, noise_draw * cell_total + cell_ids, 1024 * cell_total + cell_ids)
    extra_pick = jnp.argsort(cell_score, axis=-1)[..., :EXTRA_DEV].astype(jnp.int32)
    extra_rows = row_ids + N_ROW * (extra_pick // NB)
    extra_cols = extra_pick % NB
    devices = N_ROW * N_COL
    device_ids = jnp.arange(devices, dtype=jnp.int32).reshape(N_ROW, N_COL)
    counts = jax.random.randint(count_key, (N_ROW, N_COL), 0, EXTRA_DEV + 1, dtype=jnp.int32)
    diag_count = jnp.sum(diag_live.astype(jnp.int32), axis=-1)
    lottery = jax.random.randint(chosen_key, (N_ROW, N_COL), 0, 1024, dtype=jnp.int32) * devices + device_ids
    lottery = jnp.where(diag_count == DIAG_DEV, lottery, -1)
    chosen = jnp.argmax(lottery.reshape(-1)).astype(jnp.int32)
    counts = jnp.where(device_ids == chosen, EXTRA_DEV, counts)
    extra_live = jnp.arange(EXTRA_DEV, dtype=jnp.int32)[None, None, :] < counts[..., None]
    occupied = jnp.concatenate([diag_live, extra_live], axis=-1)
    block_rows = jnp.where(occupied, jnp.concatenate([diag_rows, extra_rows], axis=-1), -1)
    block_cols = jnp.where(occupied, jnp.concatenate([diag_rows, extra_cols], axis=-1), -1)
    shuffle_score = jax.random.randint(order_key, (N_ROW, N_COL, CAP), 0, 1024, dtype=jnp.int32) * CAP + jnp.arange(CAP, dtype=jnp.int32)[None, None, :]
    shuffle = jnp.argsort(shuffle_score, axis=-1).astype(jnp.int32)
    block_rows = jnp.take_along_axis(block_rows, shuffle, axis=-1)
    block_cols = jnp.take_along_axis(block_cols, shuffle, axis=-1)
    stacked = jnp.stack([block_rows, block_cols], axis=2)
    return jnp.transpose(stacked, (0, 2, 1, 3)).reshape(2 * N_ROW, N_COL * CAP).astype(jnp.int32)


def block_levels(stream_key, dims, pieces, low, high):
    def one(axis_at, blocks):
        draws = jax.random.uniform(jax.random.fold_in(jax.random.fold_in(stream_key, 6), axis_at), (blocks,), jnp.float32, low / len(pieces), high / len(pieces))
        return jnp.repeat(jnp.exp(draws), dims[axis_at] // blocks).reshape((-1,) + (1,) * (len(dims) - axis_at - 1))

    level = one(*pieces[0])
    for cut in pieces[1:]:
        level = level * one(*cut)
    return level


def gaussian(stream_key, shape, deviation, reach, shards=(), kind=jnp.bfloat16):
    result = deviation * jax.random.normal(stream_key, shape, jnp.float32)
    if shards:
        result = result * block_levels(stream_key, shape, shards, -0.22, 0.18)
    return jnp.clip(result, -reach, reach).astype(kind)


def setup_inputs(seed: int = 0) -> dict:
    arg_keys = jax.random.split(jax.random.key(seed), 3)
    iterate_tiles = gaussian(arg_keys[0], (N_ROW * BLK, N_COL * CAP * BLK), 0.25, 1.5, ((0, 24), (1, 32)))
    tile_blocks = draw_tile_blocks(jax.random.fold_in(arg_keys[2], 71), 0)
    return dict(iterate_tiles=iterate_tiles, tile_blocks=tile_blocks)


def partner(fold_rows, fold_cols, keep_rows, keep_cols, out_rows, out_cols):
    folded_r = fold_rows[:, None, None]
    folded_c = fold_cols[:, None, None]
    kept_r = keep_rows[None, None, :]
    kept_c = keep_cols[None, None, :]
    target_r = out_rows[None, :, None]
    target_c = out_cols[None, :, None]
    linked = (folded_r == target_r) & (folded_c == kept_r) & (kept_c == target_c)
    linked = linked & (folded_r >= 0) & (kept_r >= 0) & (target_r >= 0)
    positions = jnp.arange(keep_rows.shape[0], dtype=jnp.int32)[None, None, :]
    partner_slot = jnp.sum(jnp.where(linked, positions, 0), axis=2).astype(jnp.int32)
    return partner_slot, jnp.any(linked, axis=2)


def product(left_tiles, right_tiles, tile_blocks):
    slot_count = CAP
    left_grid = left_tiles.reshape(N_ROW, BLK, N_COL * slot_count, BLK)
    right_grid = right_tiles.reshape(N_ROW, BLK, N_COL * slot_count, BLK)
    coord_grid = tile_blocks.reshape(N_ROW, 2, N_COL * slot_count)

    def per_device(device):
        row_id = device // N_COL
        col_id = device % N_COL
        start_slot = (col_id * slot_count).astype(jnp.int32)
        left_list = jnp.transpose(left_grid[row_id], (1, 0, 2)).astype(jnp.float32)
        left_coord = coord_grid[row_id]
        right_part = lax.dynamic_slice_in_dim(right_grid, start_slot, slot_count, 2)
        right_list = jnp.transpose(right_part, (0, 2, 1, 3)).reshape(N_ROW * slot_count, BLK, BLK).astype(jnp.float32)
        right_coord = lax.dynamic_slice_in_dim(coord_grid, start_slot, slot_count, 2)
        out_coord = lax.dynamic_slice_in_dim(left_coord, start_slot, slot_count, 1)
        partner_slot, matched = partner(left_coord[0], left_coord[1], right_coord[:, 0].reshape(-1), right_coord[:, 1].reshape(-1), out_coord[0], out_coord[1])
        picked = right_list[partner_slot] * matched[:, :, None, None].astype(jnp.float32)
        return jnp.einsum('aik,aokj->oij', left_list, picked, precision=lax.Precision.HIGHEST)

    results = lax.map(per_device, jnp.arange(N_ROW * N_COL, dtype=jnp.int32))
    results = results.reshape(N_ROW, N_COL, slot_count, BLK, BLK)
    return jnp.transpose(results, (0, 3, 1, 2, 4)).reshape(N_ROW * BLK, N_COL * slot_count * BLK)


def reference(iterate_tiles, tile_blocks):
    square = product(iterate_tiles, iterate_tiles, tile_blocks).astype(jnp.bfloat16)
    cube = product(iterate_tiles, square, tile_blocks)
    used = tile_blocks.reshape(N_ROW, 2, N_COL * CAP)[:, 0] >= 0
    updated = 1.5 * iterate_tiles.astype(jnp.float32) - 0.5 * cube
    shaped = updated.reshape(N_ROW, BLK, N_COL * CAP, BLK)
    kept = jnp.where(used[:, None, :, None], shaped, jnp.zeros_like(shaped))
    return kept.reshape(N_ROW * BLK, N_COL * CAP * BLK).astype(jnp.bfloat16)
```

```python
import jax
import jax.numpy as jnp
import numpy as np
from jax import lax
from jax.experimental import pallas as pl
from jax.experimental.pallas import tpu as pltpu
from jax.sharding import Mesh, PartitionSpec as P

BLK = 128
NB = 384
ZH, Y, ZL, X, C = 3, 8, 4, 4, 2
XC = X * C
N_ROW, N_COL = ZH * Y, ZL * XC
SLOTS = 3
TILES = SLOTS * BLK
HEAD = 16
FIRST = TILES + HEAD
COLPAD = 32
SECOND = TILES + COLPAD
ROW = ("zh", "y")
COL = ("zl", "x", "c")
F32 = jnp.float32
BF16 = jnp.bfloat16
PARAMS = pltpu.CompilerParams(vmem_limit_bytes=48 * 1024 * 1024)
VMEM = pl.BlockSpec(memory_space=pltpu.VMEM)
SMEM = pl.BlockSpec(memory_space=pltpu.SMEM)


def partner(fold_rows, fold_cols, keep_rows, keep_cols, out_rows, out_cols):
    folded_r = fold_rows[:, None, None]
    folded_c = fold_cols[:, None, None]
    kept_r = keep_rows[None, None, :]
    kept_c = keep_cols[None, None, :]
    target_r = out_rows[None, :, None]
    target_c = out_cols[None, :, None]
    linked = (folded_r == target_r) & (folded_c == kept_r) & (kept_c == target_c)
    linked = linked & (folded_r >= 0) & (kept_r >= 0) & (target_r >= 0)
    positions = jnp.arange(keep_rows.shape[0], dtype=jnp.int32)[None, None, :]
    partner_slot = jnp.sum(jnp.where(linked, positions, 0), axis=2)
    return (partner_slot, jnp.any(linked, axis=2))


def columns(tile_array, tile_blocks):
    return (
        lax.all_gather(tile_array, ROW, axis=0, tiled=True),
        lax.all_gather(tile_blocks, ROW, axis=0, tiled=True),
    )


def left_fold(left_tiles, tile_blocks, panel, panel_blocks):
    block_size = left_tiles.shape[0]
    slot_count = tile_blocks.shape[1]
    panel_rows = panel.shape[0] // block_size
    right_grid = panel.reshape(panel_rows, block_size, slot_count, block_size)
    kept_blocks = panel_blocks.reshape(panel_rows, 2, slot_count)
    kept_rows = kept_blocks[:, 0].reshape(-1)
    kept_cols = kept_blocks[:, 1].reshape(-1)
    piece_tiles = lax.all_gather(left_tiles, COL, axis=1, tiled=True)
    piece_blocks = lax.all_gather(tile_blocks, COL, axis=1, tiled=True)
    piece_slots = piece_blocks.shape[1]
    left_list = piece_tiles.reshape(block_size, piece_slots, block_size)
    partner_slot, matched = partner(
        piece_blocks[0], piece_blocks[1], kept_rows, kept_cols, tile_blocks[0], tile_blocks[1]
    )
    picked = right_grid[partner_slot // slot_count, :, partner_slot % slot_count, :]
    picked = picked * matched[:, :, None, None].astype(BF16)
    running = jnp.einsum("iak,aokj->ioj", left_list, picked, preferred_element_type=F32)
    return running.reshape(block_size, slot_count * block_size)


def general(iterate_tiles, tile_blocks):
    block_size = iterate_tiles.shape[0]
    slot_count = tile_blocks.shape[1]
    panel, panel_blocks = columns(iterate_tiles, tile_blocks)
    square = left_fold(iterate_tiles, tile_blocks, panel, panel_blocks).astype(BF16)
    panel, panel_blocks = columns(square, tile_blocks)
    cube = left_fold(iterate_tiles, tile_blocks, panel, panel_blocks)
    used = tile_blocks[0] >= 0
    updated = 1.5 * iterate_tiles.astype(F32) - 0.5 * cube
    shaped = updated.reshape(block_size, slot_count, block_size)
    kept = jnp.where(used[None, :, None], shaped, jnp.zeros_like(shaped))
    return kept.reshape(block_size, slot_count * block_size).astype(BF16)


def place():
    zh, y, zl = lax.axis_index("zh"), lax.axis_index("y"), lax.axis_index("zl")
    u = lax.axis_index("x") * C + lax.axis_index("c")
    return zh, y, zl, u, zh * Y + y, zl * XC + u


def iota(shape, dim):
    return lax.broadcasted_iota(jnp.int32, shape, dim)


def dot(a, b):
    return jnp.dot(a, b, preferred_element_type=F32)


def pack_kernel(blocks, x_ref, out_ref):
    u = place()[3]
    lane = iota((HEAD, 128), 1)
    head = jnp.zeros((HEAD, 128), F32)
    for s in range(SLOTS):
        for v in range(4):
            number = blocks[v // 2, s]
            part = (number >> 4) if v % 2 == 0 else (number & 15)
            head = jnp.where(lane == v * 32 + u * SLOTS + s, part.astype(F32), head)
    head = head.astype(BF16)
    for z in range(ZH):
        for s in range(SLOTS):
            out_ref[z, s * BLK : (s + 1) * BLK, :] = x_ref[:, s * BLK : (s + 1) * BLK]
        out_ref[z, TILES:, :] = head


def plan_kernel(
    blocks, g_ref, first_ref, second_ref, p_ref, qt_ref, q_ref, imod_ref, kmod_ref, own_ref, ownc_ref,
    ybuf_ref, zbuf_ref, list_ref,
    gij_ref, gt_ref, ohi_ref, ohj_ref, dy_ref, ry_ref, dl_ref, rl_ref, list_smem, sem,
):
    zh, y, zl, u, p, q = place()
    g = g_ref[...].reshape(ZL * COLPAD, 128).astype(F32)
    g = 16.0 * g + pltpu.roll(g, 96, 1)
    row128, lane128 = iota((128, 128), 0), iota((128, 128), 1)
    g = jnp.where(((row128 & 31) < N_ROW) & ((lane128 & 63) < XC * SLOTS), g, -1.0)
    gij_ref[...] = g
    gt = g.T
    gt_ref[...] = gt
    sub = iota((NB, 128), 0).astype(F32)
    wide = iota((128, NB), 1).astype(F32)

    def onehot(mask):
        return jnp.where(mask, 1.0, 0.0).astype(BF16)

    for k in range(XC * SLOTS):
        ohi_ref[:, k * 128 : (k + 1) * 128] = onehot(sub == gt[k : k + 1, :])
        ohj_ref[k * 128 : (k + 1) * 128, :] = onehot(wide == g[:, 64 + k : 65 + k])
    adj = dot(ohi_ref[...], ohj_ref[...])
    adj_b = adj.astype(BF16)
    adj_t = adj.T.astype(BF16)
    lane = iota((1, 128), 1)
    rows = iota((32, 128), 0)
    lanes = iota((32, 128), 1)

    ci = jnp.full((1, 128), -1.0, F32)
    cj = jnp.full((1, 128), -1.0, F32)
    for s in range(SLOTS):
        shift = (s * 32 + 128 - zl * 32) & 127
        here = (lane >> 5 == s) & ((lane & 31) < N_ROW)
        rows_i = jnp.broadcast_to(gt_ref[pl.ds(u * SLOTS + s, 1), :], (8, 128))
        rows_j = jnp.broadcast_to(gt_ref[pl.ds(64 + u * SLOTS + s, 1), :], (8, 128))
        ci = jnp.where(here, pltpu.roll(rows_i, shift, 1)[0:1], ci)
        cj = jnp.where(here, pltpu.roll(rows_j, shift, 1)[0:1], cj)
    both = dot(adj_b, onehot(sub == cj)) * dot(adj_b, onehot(sub == ci))
    wanted = (dot(p_ref[...], both.astype(BF16)) > 0.5) & ((lanes & 31) != rows)
    wanted = jnp.where(wanted, 1.0, 0.0)
    dy_ref[...] = wanted
    ry_ref[...] = dot(wanted.astype(BF16), onehot((row128 < lane128) & ((row128 & 7) == (lane128 & 7))))

    li = jnp.full((1, 128), -1.0, F32)
    lk = jnp.full((1, 128), -1.0, F32)
    for z in range(ZL):
        here = (lane >> 5 == z) & ((lane & 31) < XC * SLOTS)
        mine = jnp.broadcast_to(gij_ref[pl.ds(z * COLPAD + p, 1), :], (8, 128))
        li = jnp.where(here, (pltpu.roll(mine, z * 32, 1) if z else mine)[0:1], li)
        lk = jnp.where(here, pltpu.roll(mine, (64 + z * 32) % 128, 1)[0:1], lk)
    both = dot(adj_t, onehot(sub == li)) * dot(adj_t, onehot(sub == lk))
    owner = (lanes >> 5) * XC + (((lanes & 31) * 11) >> 5)
    wanted = (dot(qt_ref[...], both.astype(BF16)) > 0.5) & (owner != rows) & ((lanes & 31) < XC * SLOTS)
    wanted = jnp.where(wanted, 1.0, 0.0)
    dl_ref[...] = wanted
    rl_ref[...] = dot(wanted.astype(BF16), onehot((row128 < lane128) & ((row128 >> 5) == (lane128 >> 5))))

    lanes8 = iota((8, 128), 1)
    rows8 = iota((8, 128), 0)
    send_d = dy_ref[pl.ds(pl.multiple_of(zh * Y, 8), 8), :]
    send_r = ry_ref[pl.ds(pl.multiple_of(zh * Y, 8), 8), :]
    ylist = jnp.zeros((8, 128), F32)
    for c in range(SLOTS):
        hit = (send_d > 0.5) & (send_r == float(c)) & ((lanes8 & 7) == y)
        code = jnp.sum(jnp.where(hit, (lanes8 + 1).astype(F32), 0.0), axis=1, keepdims=True)
        ylist = jnp.where(lanes8 == c, code, ylist)
    send_d = jnp.zeros((8, 128), F32)
    send_r = jnp.zeros((8, 128), F32)
    for z in range(ZL):
        send_d = jnp.where(rows8 == z, dl_ref[pl.ds(z * XC + u, 1), :], send_d)
        send_r = jnp.where(rows8 == z, rl_ref[pl.ds(z * XC + u, 1), :], send_r)
    zlist = jnp.zeros((8, 128), F32)
    for c in range(SLOTS):
        hit = (send_d > 0.5) & (send_r == float(c)) & ((lanes8 >> 5) == zl)
        code = jnp.sum(jnp.where(hit, ((lanes8 & 31) + 1).astype(F32), 0.0), axis=1, keepdims=True)
        zlist = jnp.where(lanes8 == c, code, zlist)

    got_d, got_r = dy_ref[pl.ds(p, 1), :], ry_ref[pl.ds(p, 1), :]
    right = jnp.where(got_d > 0.5, ((lane & 7) * SLOTS + 1).astype(F32) + got_r, 0.0)
    right = jnp.where(((lane & 31) == p) & (ci >= 0.0), (Y * SLOTS + 1 + (lane >> 5)).astype(F32), right)
    stack = jnp.where(row128 == 0, ci, jnp.where(row128 == 1, cj, right)).T
    ci_c, cj_c, right_c = stack[:, 0:1], stack[:, 1:2], stack[:, 2:3]
    linked = jnp.where(ci_c == lk, right_c, 0.0)
    meets = jnp.zeros((8, 128), F32)
    for o in range(SLOTS):
        out_i, out_j = blocks[0, o].astype(F32), blocks[1, o].astype(F32)
        met = jnp.sum(jnp.where(cj_c == out_j, linked, 0.0), axis=0, keepdims=True)
        met = jnp.where(li == out_i, met, 0.0)
        meets = jnp.where(rows8 == o, met, meets)
    got_d, got_r = dl_ref[pl.ds(q, 1), :], rl_ref[pl.ds(q, 1), :]
    terms = jnp.zeros((8, 128), F32)
    for t in range(ZL * SLOTS + SLOTS):
        if t < ZL * SLOTS:
            hit = (lane >> 5 == t // SLOTS) & (got_d > 0.5) & (got_r == float(t % SLOTS))
        else:
            hit = lane == zl * 32 + u * SLOTS + (t - ZL * SLOTS)
        value = jnp.sum(jnp.where(hit, meets, 0.0), axis=1, keepdims=True)
        terms = jnp.where(lanes8 == t, value, terms)

    most = jnp.zeros((32, 32), F32)
    from_row = jnp.where(imod_ref[...] != kmod_ref[...], adj, 0.0)
    to_col = jnp.where(ownc_ref[...] != own_ref[...], adj, 0.0).astype(BF16)
    k_lane = iota((NB, NB), 1)
    own_lane = own_ref[...] >> 3
    for c in range(Y + ZL):
        if c < Y:
            count = dot(jnp.where((k_lane & 7) == c, from_row, 0.0).astype(BF16), adj_b)
        else:
            count = dot(jnp.where(own_lane == c - Y, adj, 0.0).astype(BF16), to_col)
        count = (count * adj).astype(BF16)
        per_row = dot(p_ref[...], count)
        most = jnp.maximum(most, dot(per_row.astype(BF16), q_ref[...]))
    over = jnp.where(jnp.max(most, keepdims=True).reshape(1, 1) > SLOTS + 0.5, 1.0, 0.0)
    zlist = jnp.where((rows8 == 7) & (lanes8 == 0), over, zlist)

    list_ref[0:8, :] = ylist.astype(jnp.int32)
    list_ref[8:16, :] = zlist.astype(jnp.int32)
    list_ref[16:24, :] = terms.astype(jnp.int32)
    copy = pltpu.make_async_copy(list_ref, list_smem, sem)
    copy.start()
    copy.wait()
    pick_y(list_smem, first_ref, FIRST, ybuf_ref)
    for d in range(ZL):
        for c in range(SLOTS):
            code = list_smem[8 + d, c]

            @pl.when(code > 0)
            def _():
                k = code - 1
                src_u = (k * 11) >> 5
                start = pl.multiple_of(src_u * SECOND + (k - src_u * SLOTS) * BLK, 16)
                zbuf_ref[d, c * BLK : (c + 1) * BLK, :] = second_ref[pl.ds(start, BLK), :]


def pick_y(lists, src_ref, stride, ybuf_ref):
    for d in range(Y):
        for c in range(SLOTS):
            code = lists[d, c]

            @pl.when(code > 0)
            def _():
                r = code - 1
                start = pl.multiple_of(((r >> 3) & 3) * stride + (r >> 5) * BLK, 16)
                ybuf_ref[d, c * BLK : (c + 1) * BLK, :] = src_ref[pl.ds(start, BLK), :]


def pick_kernel(lists, src_ref, ybuf_ref):
    pick_y(lists, src_ref, TILES, ybuf_ref)


def accumulate(lists, o, acc_ref, x_ref, left_ref, own_right, right_ref):
    acc_ref[...] = jnp.zeros((BLK, BLK), F32)
    for t in range(ZL * SLOTS + SLOTS):
        code = lists[16 + o, t]
        if t < ZL * SLOTS:
            left = left_ref.at[t * BLK : (t + 1) * BLK, :]
        else:
            left = x_ref.at[:, (t - ZL * SLOTS) * BLK : (t - ZL * SLOTS + 1) * BLK]

        @pl.when((code > 0) & (code <= Y * SLOTS))
        def _():
            start = pl.multiple_of((code - 1) * BLK, BLK)
            acc_ref[...] += dot(left[...], right_ref[pl.ds(start, BLK), :])

        @pl.when(code > Y * SLOTS)
        def _():
            start = pl.multiple_of((code - 1 - Y * SLOTS) * BLK, BLK)
            acc_ref[...] += dot(left[...], own_right[pl.ds(start, BLK), :])


def square_kernel(lists, x_ref, own_ref, left_ref, right_ref, out_ref, acc_ref):
    for o in range(SLOTS):
        accumulate(lists, o, acc_ref, x_ref, left_ref, own_ref, right_ref)
        tile = acc_ref[...].astype(BF16)
        for z in range(ZH):
            out_ref[z, o * BLK : (o + 1) * BLK, :] = tile


def cube_kernel(lists, blocks, x_ref, own_ref, left_ref, right_ref, out_ref, acc_ref):
    for o in range(SLOTS):
        accumulate(lists, o, acc_ref, x_ref, left_ref, own_ref, right_ref)
        part = slice(o * BLK, (o + 1) * BLK)
        value = 1.5 * x_ref[:, part].astype(F32) - 0.5 * acc_ref[...]
        out_ref[:, part] = jnp.where(blocks[0, o] >= 0, value, 0.0).astype(BF16)


def swap(value, axes):
    return lax.all_to_all(value, axes, 0, 0, tiled=True)


def tables():
    number = np.arange(NB)
    owner = (number + number // N_ROW) % N_COL
    in_row = (number[None, :] % N_ROW == np.arange(32)[:, None]).astype(jnp.bfloat16)
    in_col = (owner[None, :] == np.arange(32)[:, None]).astype(jnp.bfloat16)
    mod = (number % N_ROW).astype(np.int32)
    owner = owner.astype(np.int32)
    return (
        in_row, in_col, np.ascontiguousarray(in_col.T),
        mod[:, None], mod[None, :], owner[None, :], owner[:, None],
    )


def per_device(x, blocks):
    first = pl.pallas_call(
        pack_kernel,
        out_shape=jax.ShapeDtypeStruct((ZH, FIRST, BLK), BF16),
        in_specs=[SMEM, VMEM], out_specs=VMEM, compiler_params=PARAMS, name="pack",
    )(blocks, x)
    own = first[0, :TILES]
    first = swap(first, "zh")
    heads = jnp.pad(first[:, TILES], ((0, HEAD - ZH), (0, 0)))
    heads = swap(jnp.broadcast_to(heads[None], (Y, HEAD, 128)).reshape(Y * HEAD, 128), "y")
    heads = heads.reshape(Y, HEAD, 128)[:, :ZH].transpose(1, 0, 2).reshape(N_ROW, 128)
    heads = jnp.pad(heads, ((0, COLPAD - N_ROW), (0, 0)))
    second = lax.all_gather(jnp.concatenate([own, heads], axis=0), ("x", "c"), axis=0)
    heads = jnp.sum(second[:, TILES:].astype(F32), axis=0).astype(BF16)
    heads = swap(jnp.broadcast_to(heads[None], (ZL, COLPAD, 128)).reshape(ZL * COLPAD, 128), "zl")
    ybuf, zbuf, lists = pl.pallas_call(
        plan_kernel,
        out_shape=(
            jax.ShapeDtypeStruct((Y, TILES, BLK), BF16),
            jax.ShapeDtypeStruct((ZL, TILES, BLK), BF16),
            jax.ShapeDtypeStruct((24, 128), jnp.int32),
        ),
        in_specs=[SMEM] + [VMEM] * 10, out_specs=(VMEM,) * 3,
        scratch_shapes=[
            pltpu.VMEM((128, 128), F32), pltpu.VMEM((128, 128), F32),
            pltpu.VMEM((NB, XC * SLOTS * 128), BF16), pltpu.VMEM((XC * SLOTS * 128, NB), BF16),
            pltpu.VMEM((32, 128), F32), pltpu.VMEM((32, 128), F32),
            pltpu.VMEM((32, 128), F32), pltpu.VMEM((32, 128), F32),
            pltpu.SMEM((24, 128), jnp.int32), pltpu.SemaphoreType.DMA,
        ],
        compiler_params=PARAMS, name="plan",
    )(
        blocks, heads.reshape(ZL, COLPAD, 128), first.reshape(ZH * FIRST, BLK),
        second.reshape(XC * SECOND, BLK), *[jnp.asarray(t) for t in tables()],
    )
    left = swap(zbuf, "zl").reshape(ZL * TILES, BLK)
    right = swap(ybuf, "y").reshape(Y * TILES, BLK)
    square = pl.pallas_call(
        square_kernel,
        out_shape=jax.ShapeDtypeStruct((ZH, TILES, BLK), BF16),
        in_specs=[SMEM] + [VMEM] * 4, out_specs=VMEM,
        scratch_shapes=[pltpu.VMEM((BLK, BLK), F32)], compiler_params=PARAMS, name="square",
    )(lists, x, own, left, right)
    own_square = square[0]
    square = swap(square, "zh")
    ybuf = pl.pallas_call(
        pick_kernel,
        out_shape=jax.ShapeDtypeStruct((Y, TILES, BLK), BF16),
        in_specs=[SMEM, VMEM], out_specs=VMEM, compiler_params=PARAMS, name="pick",
    )(lists, square.reshape(ZH * TILES, BLK))
    right = swap(ybuf, "y").reshape(Y * TILES, BLK)
    result = pl.pallas_call(
        cube_kernel,
        out_shape=jax.ShapeDtypeStruct(x.shape, BF16),
        in_specs=[SMEM, SMEM] + [VMEM] * 4, out_specs=VMEM,
        scratch_shapes=[pltpu.VMEM((BLK, BLK), F32)], compiler_params=PARAMS, name="cube",
    )(lists, blocks, x, own_square, left, right)
    return lax.cond(lists[15, 0] > 0, lambda: general(x, blocks), lambda: result)


def solution(mesh):
    fine = Mesh(mesh.devices.reshape(ZH, Y, ZL, X, C), ROW + COL)
    return jax.shard_map(
        per_device,
        mesh=fine,
        in_specs=(P(ROW, COL), P(ROW, COL)),
        out_specs=P(ROW, COL),
        check_vma=False,
    )
```

```python
import jax
import jax.numpy as jnp
from jax import lax
from jax.experimental import pallas as pl
from jax.experimental.pallas import tpu as pltpu
from jax.sharding import Mesh, PartitionSpec as P

BLK = 128
NB = 384
ZH, Y, ZL, X, C = 3, 8, 4, 4, 2
XC = X * C
N_ROW, N_COL = ZH * Y, ZL * XC
SLOTS = 3
TILES = SLOTS * BLK
HEAD = 32
PANEL = TILES + HEAD
SLOTS_ROW = XC * SLOTS
LEFTS = ZL * SLOTS + SLOTS
OWN, PLAIN = 128, 160
ZLIST, TERMS = 32, 40
ROW = ("zh", "y")
COL = ("zl", "x", "c")
F32 = jnp.float32
BF16 = jnp.bfloat16
PARAMS = pltpu.CompilerParams(vmem_limit_bytes=48 * 1024 * 1024)
VMEM = pl.BlockSpec(memory_space=pltpu.VMEM)
SMEM = pl.BlockSpec(memory_space=pltpu.SMEM)


def partner(fold_rows, fold_cols, keep_rows, keep_cols, out_rows, out_cols):
    folded_r = fold_rows[:, None, None]
    folded_c = fold_cols[:, None, None]
    kept_r = keep_rows[None, None, :]
    kept_c = keep_cols[None, None, :]
    target_r = out_rows[None, :, None]
    target_c = out_cols[None, :, None]
    linked = (folded_r == target_r) & (folded_c == kept_r) & (kept_c == target_c)
    linked = linked & (folded_r >= 0) & (kept_r >= 0) & (target_r >= 0)
    positions = jnp.arange(keep_rows.shape[0], dtype=jnp.int32)[None, None, :]
    partner_slot = jnp.sum(jnp.where(linked, positions, 0), axis=2)
    return (partner_slot, jnp.any(linked, axis=2))


def columns(tile_array, tile_blocks):
    return (
        lax.all_gather(tile_array, ROW, axis=0, tiled=True),
        lax.all_gather(tile_blocks, ROW, axis=0, tiled=True),
    )


def left_fold(left_tiles, tile_blocks, panel, panel_blocks):
    block_size = left_tiles.shape[0]
    slot_count = tile_blocks.shape[1]
    panel_rows = panel.shape[0] // block_size
    right_grid = panel.reshape(panel_rows, block_size, slot_count, block_size)
    kept_blocks = panel_blocks.reshape(panel_rows, 2, slot_count)
    kept_rows = kept_blocks[:, 0].reshape(-1)
    kept_cols = kept_blocks[:, 1].reshape(-1)
    piece_tiles = lax.all_gather(left_tiles, COL, axis=1, tiled=True)
    piece_blocks = lax.all_gather(tile_blocks, COL, axis=1, tiled=True)
    piece_slots = piece_blocks.shape[1]
    left_list = piece_tiles.reshape(block_size, piece_slots, block_size)
    partner_slot, matched = partner(
        piece_blocks[0], piece_blocks[1], kept_rows, kept_cols, tile_blocks[0], tile_blocks[1]
    )
    picked = right_grid[partner_slot // slot_count, :, partner_slot % slot_count, :]
    picked = picked * matched[:, :, None, None].astype(BF16)
    running = jnp.einsum("iak,aokj->ioj", left_list, picked, preferred_element_type=F32)
    return running.reshape(block_size, slot_count * block_size)


def general(iterate_tiles, tile_blocks):
    block_size = iterate_tiles.shape[0]
    slot_count = tile_blocks.shape[1]
    panel, panel_blocks = columns(iterate_tiles, tile_blocks)
    square = left_fold(iterate_tiles, tile_blocks, panel, panel_blocks).astype(BF16)
    panel, panel_blocks = columns(square, tile_blocks)
    cube = left_fold(iterate_tiles, tile_blocks, panel, panel_blocks)
    used = tile_blocks[0] >= 0
    updated = 1.5 * iterate_tiles.astype(F32) - 0.5 * cube
    shaped = updated.reshape(block_size, slot_count, block_size)
    kept = jnp.where(used[None, :, None], shaped, jnp.zeros_like(shaped))
    return kept.reshape(block_size, slot_count * block_size).astype(BF16)


def place():
    zh, y, zl = lax.axis_index("zh"), lax.axis_index("y"), lax.axis_index("zl")
    u = lax.axis_index("x") * C + lax.axis_index("c")
    return zh, y, zl, u, zh * Y + y, zl * XC + u


def iota(shape, dim):
    return lax.broadcasted_iota(jnp.int32, shape, dim)


def dot(a, b):
    return jnp.dot(a, b, preferred_element_type=F32)


def onehot(mask):
    return jnp.where(mask, 1.0, 0.0).astype(BF16)


def row_of(number):
    return number - N_ROW * ((number * 683) >> 14)


def col_of(number):
    return (number + ((number * 683) >> 14)) & (N_COL - 1)


def pack_kernel(blocks, x_ref, out_ref, own_ref):
    zh, y, zl, u, p, q = place()
    lane = iota((HEAD, 128), 1)
    here = iota((HEAD, 128), 0) == p
    head = jnp.zeros((HEAD, 128), F32)
    for s in range(SLOTS):
        for v in range(4):
            number = blocks[v // 2, s]
            part = (number >> 4) if v % 2 == 0 else (number & 15)
            head = jnp.where(here & (lane == v * 32 + u * SLOTS + s), part.astype(F32), head)
    head = head.astype(BF16)
    for s in range(SLOTS):
        tile = x_ref[:, s * BLK : (s + 1) * BLK]
        own_ref[s * BLK : (s + 1) * BLK, :] = tile
        for z in range(ZH):
            out_ref[z, s * BLK : (s + 1) * BLK, :] = tile
    for z in range(ZH):
        out_ref[z, TILES:, :] = head


def plan_kernel(
    blocks, g_ref, second_ref, zbuf_ref, list_ref,
    gij_ref, gt_ref, ohi_ref, ohj_ref, dl_ref, rl_ref, list_smem, sem,
):
    zh, y, zl, u, p, q = place()
    g = jnp.sum(g_ref[...].astype(F32), axis=0)
    g = 16.0 * g + pltpu.roll(g, 96, 1)
    row128, lane128 = iota((128, 128), 0), iota((128, 128), 1)
    g = jnp.where(((row128 & 31) < N_ROW) & ((lane128 & 63) < SLOTS_ROW), g, -1.0)
    gij_ref[...] = g
    gt = g.T
    gt_ref[...] = gt
    sub = iota((NB, 128), 0).astype(F32)
    wide = iota((128, NB), 1).astype(F32)
    for k in range(SLOTS_ROW):
        ohi_ref[:, k * 128 : (k + 1) * 128] = onehot(sub == gt[k : k + 1, :])
        ohj_ref[k * 128 : (k + 1) * 128, :] = onehot(wide == g[:, 64 + k : 65 + k])
    adj = dot(ohi_ref[...], ohj_ref[...])
    adj_b = adj.astype(BF16)
    adj_tf = adj.T
    adj_t = adj_tf.astype(BF16)
    mutual = adj * adj_tf
    lane = iota((1, 128), 1)
    rows = iota((32, 128), 0)
    lanes = iota((32, 128), 1)
    number = iota((32, NB), 1)
    in_row = onehot(row_of(number) == iota((32, NB), 0))
    in_col = onehot(col_of(number) == iota((32, NB), 0))
    in_col_t = onehot(col_of(iota((NB, 32), 0)) == iota((NB, 32), 1))

    ci = jnp.full((1, 128), -1.0, F32)
    cj = jnp.full((1, 128), -1.0, F32)
    for s in range(SLOTS):
        shift = (s * 32 + 128 - zl * 32) & 127
        here = (lane >> 5 == s) & ((lane & 31) < N_ROW)
        rows_i = jnp.broadcast_to(gt_ref[pl.ds(u * SLOTS + s, 1), :], (8, 128))
        rows_j = jnp.broadcast_to(gt_ref[pl.ds(64 + u * SLOTS + s, 1), :], (8, 128))
        ci = jnp.where(here, pltpu.roll(rows_i, shift, 1)[0:1], ci)
        cj = jnp.where(here, pltpu.roll(rows_j, shift, 1)[0:1], cj)
    of_i = onehot(sub == ci)
    both = dot(adj_b, onehot(sub == cj)) * dot(adj_b, of_i)
    pairs = jnp.broadcast_to(jnp.sum(mutual, axis=0, keepdims=True), (8, NB)).astype(BF16)
    plain = (ci == cj) & (ci >= 0.0) & (dot(pairs, of_i)[0:1] < 1.5)
    plain_f = jnp.where(plain, 1.0, 0.0)
    wanted = (dot(in_row, both.astype(BF16)) > 0.5) & ((lanes & 31) != rows) & (plain_f < 0.5)
    hit = wanted & ((lanes & 31) == p)
    code = jnp.sum(jnp.where(hit, ((lanes >> 5) + 1).astype(F32), 0.0), axis=1, keepdims=True)
    sends = jnp.where(lanes == 0, code, 0.0)

    li = jnp.full((1, 128), -1.0, F32)
    lk = jnp.full((1, 128), -1.0, F32)
    for z in range(ZL):
        here = (lane >> 5 == z) & ((lane & 31) < SLOTS_ROW)
        mine = jnp.broadcast_to(gij_ref[pl.ds(z * 32 + p, 1), :], (8, 128))
        li = jnp.where(here, (pltpu.roll(mine, z * 32, 1) if z else mine)[0:1], li)
        lk = jnp.where(here, pltpu.roll(mine, (64 + z * 32) % 128, 1)[0:1], lk)
    both = dot(adj_t, onehot(sub == li)) * dot(adj_t, onehot(sub == lk))
    owner = (lanes >> 5) * XC + (((lanes & 31) * 11) >> 5)
    wanted = (dot(in_col, both.astype(BF16)) > 0.5) & (owner != rows) & ((lanes & 31) < SLOTS_ROW)
    wanted = jnp.where(wanted, 1.0, 0.0)
    dl_ref[...] = wanted
    rl_ref[...] = dot(wanted.astype(BF16), onehot((row128 < lane128) & ((row128 >> 5) == (lane128 >> 5))))
    lanes8 = iota((8, 128), 1)
    rows8 = iota((8, 128), 0)
    send_d = jnp.zeros((8, 128), F32)
    send_r = jnp.zeros((8, 128), F32)
    for z in range(ZL):
        send_d = jnp.where(rows8 == z, dl_ref[pl.ds(z * XC + u, 1), :], send_d)
        send_r = jnp.where(rows8 == z, rl_ref[pl.ds(z * XC + u, 1), :], send_r)
    zlist = jnp.zeros((8, 128), F32)
    for c in range(SLOTS):
        hit = (send_d > 0.5) & (send_r == float(c)) & ((lanes8 >> 5) == zl)
        code = jnp.sum(jnp.where(hit, ((lanes8 & 31) + 1).astype(F32), 0.0), axis=1, keepdims=True)
        zlist = jnp.where(lanes8 == c, code, zlist)

    right = jnp.where(ci >= 0.0, (lane + 1).astype(F32), 0.0)
    again = jnp.where(plain, float(PLAIN), right)
    again = jnp.where(((lane & 31) == p) & (ci >= 0.0), (OWN + (lane >> 5)).astype(F32), again)
    stack = jnp.where(row128 == 0, ci, jnp.where(row128 == 1, cj, jnp.where(row128 == 2, right, again))).T
    ci_c, cj_c = stack[:, 0:1], stack[:, 1:2]
    met_c = ci_c == lk
    linked = (jnp.where(met_c, stack[:, 2:3], 0.0), jnp.where(met_c, stack[:, 3:4], 0.0))
    meets = [jnp.zeros((8, 128), F32), jnp.zeros((8, 128), F32)]
    terms = jnp.zeros((8, 128), F32)
    for o in range(SLOTS):
        out_i, out_j = blocks[0, o].astype(F32), blocks[1, o].astype(F32)
        for n in range(2):
            met = jnp.sum(jnp.where(cj_c == out_j, linked[n], 0.0), axis=0, keepdims=True)
            meets[n] = jnp.where(rows8 == o, jnp.where(li == out_i, met, 0.0), meets[n])
        hit = plain & (ci == out_j) & ((lane & 31) != p)
        code = jnp.sum(jnp.where(hit, (lane + 1).astype(F32), 0.0), axis=1, keepdims=True)
        terms = jnp.where((rows8 == o) & (lanes8 == 64), code, terms)
    got_d, got_r = dl_ref[pl.ds(q, 1), :], rl_ref[pl.ds(q, 1), :]
    for t in range(LEFTS):
        if t < ZL * SLOTS:
            hit = (lane >> 5 == t // SLOTS) & (got_d > 0.5) & (got_r == float(t % SLOTS))
        else:
            hit = lane == zl * 32 + u * SLOTS + (t - ZL * SLOTS)
        for n in range(2):
            value = jnp.sum(jnp.where(hit, meets[n], 0.0), axis=1, keepdims=True)
            terms = jnp.where(lanes8 == n * 32 + t, value, terms)

    def per_dev(count):
        return dot(dot(in_row, (count * adj).astype(BF16)).astype(BF16), in_col_t)

    from_i, from_k = iota((NB, NB), 0), iota((NB, NB), 1)
    k_row = row_of(iota((1, NB), 1))
    k_col = col_of(iota((1, NB), 1))
    i_row = row_of(iota((NB, 1), 0))
    i_col = col_of(iota((NB, 1), 0))
    most = jnp.zeros((32, 32), F32)
    to_col = jnp.where(i_col != k_col, adj, 0.0).astype(BF16)
    for z in range(ZL):
        part = jnp.where((k_col >> 3) == z, adj, 0.0).astype(BF16)
        most = jnp.maximum(most, per_dev(dot(part, to_col)))
    left_over = jnp.max(most, keepdims=True) > SLOTS + 0.5
    moving = jnp.where(i_row != k_row, adj, 0.0)
    single = jnp.sum(mutual, axis=1, keepdims=True) < 1.5
    target = jnp.where((from_i == from_k) & single, 0.0, adj).astype(BF16)
    square_row = k_row * k_row
    n, first, high, low = (
        per_dev(dot((moving * weight.astype(F32)).astype(BF16), target))
        for weight in (k_row * 0 + 1, k_row, square_row >> 4, square_row & 15)
    )
    clash = (n > 2.5) | ((n > 1.5) & (2.0 * (16.0 * high + low) == first * first))
    clash = jnp.max(jnp.where(clash, 1.0, 0.0), keepdims=True)
    level = jnp.where(left_over, 2.0, clash)
    zlist = jnp.where((rows8 == 7) & (lanes8 == 0), level, zlist)

    list_ref[0:ZLIST, :] = sends.astype(jnp.int32)
    list_ref[ZLIST:TERMS, :] = zlist.astype(jnp.int32)
    list_ref[TERMS:, :] = terms.astype(jnp.int32)
    copy = pltpu.make_async_copy(list_ref, list_smem, sem)
    copy.start()
    copy.wait()
    for d in range(ZL):
        for c in range(SLOTS):
            code = list_smem[ZLIST + d, c]

            @pl.when(code > 0)
            def _():
                k = code - 1
                src_u = (k * 11) >> 5
                start = pl.multiple_of(src_u * PANEL + (k - src_u * SLOTS) * BLK, 16)
                zbuf_ref[d, c * BLK : (c + 1) * BLK, :] = second_ref[pl.ds(start, BLK), :]


def tile_at(start):
    return pl.ds(pl.multiple_of(start, 16), BLK)


def left_at(t, left_ref, own_ref):
    if t < ZL * SLOTS:
        return left_ref.at[t * BLK : (t + 1) * BLK, :]
    t -= ZL * SLOTS
    return own_ref.at[t * BLK : (t + 1) * BLK, :]


def panel_start(code):
    r = code - 1
    return ((r & 7) * ZH + ((r >> 3) & 3)) * PANEL + (r >> 5) * BLK


def square_kernel(lists, own_ref, left_ref, right_ref, out_ref, diag_ref, send_ref, acc_ref):
    for o in range(SLOTS):
        part = slice(o * BLK, (o + 1) * BLK)
        acc_ref[...] = jnp.zeros((BLK, BLK), F32)
        for t in range(LEFTS):
            code = lists[TERMS + o, t]
            left = left_at(t, left_ref, own_ref)

            @pl.when(code > 0)
            def _():
                acc_ref[...] += dot(left[...], right_ref[tile_at(panel_start(code)), :])

        out_ref[part, :] = acc_ref[...].astype(BF16)
        code = lists[TERMS + o, 64]

        @pl.when(code > 0)
        def _():
            tile = right_ref[tile_at(panel_start(code)), :]
            diag_ref[part, :] = dot(tile, tile).astype(BF16)

    for d in range(N_ROW):
        code = lists[d, 0]

        @pl.when((code > 0) & (code <= SLOTS))
        def _():
            send_ref[d * BLK : (d + 1) * BLK, :] = out_ref[tile_at((code - 1) * BLK), :]


def cube_kernel(room, lists, blocks, own_ref, left_ref, square_ref, diag_ref, right_ref, out_ref, acc_ref):
    for o in range(SLOTS):
        part = slice(o * BLK, (o + 1) * BLK)
        acc_ref[...] = jnp.zeros((BLK, BLK), F32)
        for t in range(LEFTS):
            code = lists[TERMS + o, 32 + t]
            left = left_at(t, left_ref, own_ref)

            @pl.when((code > 0) & (code < OWN))
            def _():
                r = code - 1
                start = (r & 31) * BLK if room == 1 else ((r & 31) * SLOTS + (r >> 5)) * BLK
                acc_ref[...] += dot(left[...], right_ref[tile_at(start), :])

            @pl.when((code >= OWN) & (code < PLAIN))
            def _():
                acc_ref[...] += dot(left[...], square_ref[tile_at((code - OWN) * BLK), :])

            @pl.when(code == PLAIN)
            def _():
                acc_ref[...] += dot(left[...], diag_ref[part, :])

        value = 1.5 * own_ref[part, :].astype(F32) - 0.5 * acc_ref[...]
        out_ref[:, part] = jnp.where(blocks[0, o] >= 0, value, 0.0).astype(BF16)


def swap(value, axes):
    return lax.all_to_all(value, axes, 0, 0, tiled=True)


def like(*shape, dtype=BF16):
    return jax.ShapeDtypeStruct(shape, dtype)


def per_device(x, blocks):
    first, own = pl.pallas_call(
        pack_kernel,
        out_shape=(like(ZH, PANEL, BLK), like(TILES, BLK)),
        in_specs=[SMEM, VMEM], out_specs=(VMEM, VMEM), compiler_params=PARAMS, name="pack",
    )(blocks, x)
    first = swap(first, "zh")
    right = lax.all_gather(first.reshape(ZH * PANEL, BLK), "y", axis=0, tiled=True)
    heads = jnp.sum(first[:, TILES:].astype(F32), axis=0).astype(BF16)
    second = lax.all_gather(jnp.concatenate([own, heads], axis=0), ("x", "c"), axis=0)
    heads = jnp.sum(second[:, TILES:].astype(F32), axis=0).astype(BF16)
    heads = jnp.broadcast_to(heads[None], (Y * ZL, HEAD, 128)).reshape(Y * ZL * HEAD, 128)
    heads = swap(heads, ("y", "zl")).reshape(Y, ZL * HEAD, 128)
    zbuf, lists = pl.pallas_call(
        plan_kernel,
        out_shape=(like(ZL, TILES, BLK), like(TERMS + 8, 128, dtype=jnp.int32)),
        in_specs=[SMEM, VMEM, VMEM], out_specs=(VMEM, VMEM),
        scratch_shapes=[
            pltpu.VMEM((128, 128), F32), pltpu.VMEM((128, 128), F32),
            pltpu.VMEM((NB, SLOTS_ROW * 128), BF16), pltpu.VMEM((SLOTS_ROW * 128, NB), BF16),
            pltpu.VMEM((32, 128), F32), pltpu.VMEM((32, 128), F32),
            pltpu.SMEM((TERMS + 8, 128), jnp.int32), pltpu.SemaphoreType.DMA,
        ],
        compiler_params=PARAMS, name="plan",
    )(blocks, heads, second.reshape(XC * PANEL, BLK))
    left = swap(zbuf, "zl").reshape(ZL * TILES, BLK)
    square, diag, send = pl.pallas_call(
        square_kernel,
        out_shape=(like(TILES, BLK), like(TILES, BLK), like(N_ROW * BLK, BLK)),
        in_specs=[SMEM] + [VMEM] * 3, out_specs=(VMEM,) * 3,
        scratch_shapes=[pltpu.VMEM((BLK, BLK), F32)], compiler_params=PARAMS, name="square",
    )(lists, own, left, right)

    def finish(room, squares):
        return pl.pallas_call(
            lambda *refs: cube_kernel(room, *refs),
            out_shape=like(*x.shape),
            in_specs=[SMEM, SMEM] + [VMEM] * 5, out_specs=VMEM,
            scratch_shapes=[pltpu.VMEM((BLK, BLK), F32)], compiler_params=PARAMS, name="cube%d" % room,
        )(lists, blocks, own, left, square, diag, squares)

    def roomy():
        return finish(SLOTS, swap(jnp.tile(square, (N_ROW, 1)), ROW))

    result = finish(1, swap(send, ROW))
    return lax.switch(lists[TERMS - 1, 0], [lambda: result, roomy, lambda: general(x, blocks)])


def solution(mesh):
    fine = Mesh(mesh.devices.reshape(ZH, Y, ZL, X, C), ROW + COL)
    return jax.shard_map(
        per_device,
        mesh=fine,
        in_specs=(P(ROW, COL), P(ROW, COL)),
        out_specs=P(ROW, COL),
        check_vma=False,
    )
```

```python
import jax
import jax.numpy as jnp
from jax import lax
from jax.experimental import pallas as pl
from jax.experimental.pallas import tpu as pltpu
from jax.sharding import Mesh, PartitionSpec as P

BLK = 128
NB = 384
ZH, Y, ZL, X, C = 3, 8, 4, 4, 2
XC = X * C
N_ROW, N_COL = ZH * Y, ZL * XC
SLOTS = 3
TILES = SLOTS * BLK
HEAD = 16
PANEL = TILES + HEAD
SLOTS_ROW = XC * SLOTS
LEFTS = ZL * SLOTS + SLOTS
OWN, PLAIN = 128, 160
ZLIST, TERMS = 32, 40
ROW = ("zh", "y")
COL = ("zl", "x", "c")
F32 = jnp.float32
BF16 = jnp.bfloat16
PARAMS = pltpu.CompilerParams(vmem_limit_bytes=48 * 1024 * 1024)
VMEM = pl.BlockSpec(memory_space=pltpu.VMEM)
SMEM = pl.BlockSpec(memory_space=pltpu.SMEM)


def partner(fold_rows, fold_cols, keep_rows, keep_cols, out_rows, out_cols):
    folded_r = fold_rows[:, None, None]
    folded_c = fold_cols[:, None, None]
    kept_r = keep_rows[None, None, :]
    kept_c = keep_cols[None, None, :]
    target_r = out_rows[None, :, None]
    target_c = out_cols[None, :, None]
    linked = (folded_r == target_r) & (folded_c == kept_r) & (kept_c == target_c)
    linked = linked & (folded_r >= 0) & (kept_r >= 0) & (target_r >= 0)
    positions = jnp.arange(keep_rows.shape[0], dtype=jnp.int32)[None, None, :]
    partner_slot = jnp.sum(jnp.where(linked, positions, 0), axis=2)
    return (partner_slot, jnp.any(linked, axis=2))


def columns(tile_array, tile_blocks):
    return (
        lax.all_gather(tile_array, ROW, axis=0, tiled=True),
        lax.all_gather(tile_blocks, ROW, axis=0, tiled=True),
    )


def left_fold(left_tiles, tile_blocks, panel, panel_blocks):
    block_size = left_tiles.shape[0]
    slot_count = tile_blocks.shape[1]
    panel_rows = panel.shape[0] // block_size
    right_grid = panel.reshape(panel_rows, block_size, slot_count, block_size)
    kept_blocks = panel_blocks.reshape(panel_rows, 2, slot_count)
    kept_rows = kept_blocks[:, 0].reshape(-1)
    kept_cols = kept_blocks[:, 1].reshape(-1)
    piece_tiles = lax.all_gather(left_tiles, COL, axis=1, tiled=True)
    piece_blocks = lax.all_gather(tile_blocks, COL, axis=1, tiled=True)
    piece_slots = piece_blocks.shape[1]
    left_list = piece_tiles.reshape(block_size, piece_slots, block_size)
    partner_slot, matched = partner(
        piece_blocks[0], piece_blocks[1], kept_rows, kept_cols, tile_blocks[0], tile_blocks[1]
    )
    picked = right_grid[partner_slot // slot_count, :, partner_slot % slot_count, :]
    picked = picked * matched[:, :, None, None].astype(BF16)
    running = jnp.einsum("iak,aokj->ioj", left_list, picked, preferred_element_type=F32)
    return running.reshape(block_size, slot_count * block_size)


def general(iterate_tiles, tile_blocks):
    block_size = iterate_tiles.shape[0]
    slot_count = tile_blocks.shape[1]
    panel, panel_blocks = columns(iterate_tiles, tile_blocks)
    square = left_fold(iterate_tiles, tile_blocks, panel, panel_blocks).astype(BF16)
    panel, panel_blocks = columns(square, tile_blocks)
    cube = left_fold(iterate_tiles, tile_blocks, panel, panel_blocks)
    used = tile_blocks[0] >= 0
    updated = 1.5 * iterate_tiles.astype(F32) - 0.5 * cube
    shaped = updated.reshape(block_size, slot_count, block_size)
    kept = jnp.where(used[None, :, None], shaped, jnp.zeros_like(shaped))
    return kept.reshape(block_size, slot_count * block_size).astype(BF16)


def place():
    zh, y, zl = lax.axis_index("zh"), lax.axis_index("y"), lax.axis_index("zl")
    u = lax.axis_index("x") * C + lax.axis_index("c")
    return zh, y, zl, u, zh * Y + y, zl * XC + u


def iota(shape, dim):
    return lax.broadcasted_iota(jnp.int32, shape, dim)


def dot(a, b):
    return jnp.dot(a, b, preferred_element_type=F32)


def onehot(mask):
    return jnp.where(mask, 1.0, 0.0).astype(BF16)


def row_of(number):
    return number - N_ROW * ((number * 683) >> 14)


def col_of(number):
    return (number + ((number * 683) >> 14)) & (N_COL - 1)


def pack_kernel(blocks, x_ref, out_ref, own_ref):
    zh, y, zl, u, p, q = place()
    lane = iota((HEAD, 128), 1)
    here = iota((HEAD, 128), 0) == zh
    head = jnp.zeros((HEAD, 128), F32)
    for s in range(SLOTS):
        for v in range(4):
            number = blocks[v // 2, s]
            part = (number >> 4) if v % 2 == 0 else (number & 15)
            head = jnp.where(here & (lane == v * 32 + u * SLOTS + s), part.astype(F32), head)
    head = head.astype(BF16)
    for s in range(SLOTS):
        tile = x_ref[:, s * BLK : (s + 1) * BLK]
        own_ref[s * BLK : (s + 1) * BLK, :] = tile
        for z in range(ZH):
            out_ref[z, s * BLK : (s + 1) * BLK, :] = tile
    for z in range(ZH):
        out_ref[z, TILES:, :] = head


def plan_kernel(
    blocks, g_ref, second_ref, zbuf_ref, list_ref,
    gij_ref, gt_ref, ohi_ref, ohj_ref, dl_ref, rl_ref, list_smem, sem,
):
    zh, y, zl, u, p, q = place()
    told = g_ref[...].astype(F32)
    for z in range(ZL):
        for h in range(ZH):
            gij_ref[z * 32 + h * Y : z * 32 + (h + 1) * Y, :] = told[:, z * HEAD + h, :]
        gij_ref[z * 32 + N_ROW : (z + 1) * 32, :] = jnp.zeros((32 - N_ROW, 128), F32)
    g = gij_ref[...]
    g = 16.0 * g + pltpu.roll(g, 96, 1)
    row128, lane128 = iota((128, 128), 0), iota((128, 128), 1)
    g = jnp.where(((row128 & 31) < N_ROW) & ((lane128 & 63) < SLOTS_ROW), g, -1.0)
    gij_ref[...] = g
    gt = g.T
    gt_ref[...] = gt
    sub = iota((NB, 128), 0).astype(F32)
    wide = iota((128, NB), 1).astype(F32)
    for k in range(SLOTS_ROW):
        ohi_ref[:, k * 128 : (k + 1) * 128] = onehot(sub == gt[k : k + 1, :])
        ohj_ref[k * 128 : (k + 1) * 128, :] = onehot(wide == g[:, 64 + k : 65 + k])
    adj = dot(ohi_ref[...], ohj_ref[...])
    adj_b = adj.astype(BF16)
    adj_tf = adj.T
    adj_t = adj_tf.astype(BF16)
    mutual = adj * adj_tf
    lane = iota((1, 128), 1)
    rows = iota((32, 128), 0)
    lanes = iota((32, 128), 1)
    number = iota((32, NB), 1)
    in_row = onehot(row_of(number) == iota((32, NB), 0))
    in_col = onehot(col_of(number) == iota((32, NB), 0))
    in_col_t = onehot(col_of(iota((NB, 32), 0)) == iota((NB, 32), 1))

    ci = jnp.full((1, 128), -1.0, F32)
    cj = jnp.full((1, 128), -1.0, F32)
    for s in range(SLOTS):
        shift = (s * 32 + 128 - zl * 32) & 127
        here = (lane >> 5 == s) & ((lane & 31) < N_ROW)
        rows_i = jnp.broadcast_to(gt_ref[pl.ds(u * SLOTS + s, 1), :], (8, 128))
        rows_j = jnp.broadcast_to(gt_ref[pl.ds(64 + u * SLOTS + s, 1), :], (8, 128))
        ci = jnp.where(here, pltpu.roll(rows_i, shift, 1)[0:1], ci)
        cj = jnp.where(here, pltpu.roll(rows_j, shift, 1)[0:1], cj)
    of_i = onehot(sub == ci)
    both = dot(adj_b, onehot(sub == cj)) * dot(adj_b, of_i)
    pairs = jnp.broadcast_to(jnp.sum(mutual, axis=0, keepdims=True), (8, NB)).astype(BF16)
    plain = (ci == cj) & (ci >= 0.0) & (dot(pairs, of_i)[0:1] < 1.5)
    plain_f = jnp.where(plain, 1.0, 0.0)
    wanted = (dot(in_row, both.astype(BF16)) > 0.5) & ((lanes & 31) != rows) & (plain_f < 0.5)
    hit = wanted & ((lanes & 31) == p)
    code = jnp.sum(jnp.where(hit, ((lanes >> 5) + 1).astype(F32), 0.0), axis=1, keepdims=True)
    sends = jnp.where(lanes == 0, code, 0.0)

    li = jnp.full((1, 128), -1.0, F32)
    lk = jnp.full((1, 128), -1.0, F32)
    for z in range(ZL):
        here = (lane >> 5 == z) & ((lane & 31) < SLOTS_ROW)
        mine = jnp.broadcast_to(gij_ref[pl.ds(z * 32 + p, 1), :], (8, 128))
        li = jnp.where(here, (pltpu.roll(mine, z * 32, 1) if z else mine)[0:1], li)
        lk = jnp.where(here, pltpu.roll(mine, (64 + z * 32) % 128, 1)[0:1], lk)
    both = dot(adj_t, onehot(sub == li)) * dot(adj_t, onehot(sub == lk))
    owner = (lanes >> 5) * XC + (((lanes & 31) * 11) >> 5)
    wanted = (dot(in_col, both.astype(BF16)) > 0.5) & (owner != rows) & ((lanes & 31) < SLOTS_ROW)
    wanted = jnp.where(wanted, 1.0, 0.0)
    dl_ref[...] = wanted
    rl_ref[...] = dot(wanted.astype(BF16), onehot((row128 < lane128) & ((row128 >> 5) == (lane128 >> 5))))
    lanes8 = iota((8, 128), 1)
    rows8 = iota((8, 128), 0)
    send_d = jnp.zeros((8, 128), F32)
    send_r = jnp.zeros((8, 128), F32)
    for z in range(ZL):
        send_d = jnp.where(rows8 == z, dl_ref[pl.ds(z * XC + u, 1), :], send_d)
        send_r = jnp.where(rows8 == z, rl_ref[pl.ds(z * XC + u, 1), :], send_r)
    zlist = jnp.zeros((8, 128), F32)
    for c in range(SLOTS):
        hit = (send_d > 0.5) & (send_r == float(c)) & ((lanes8 >> 5) == zl)
        code = jnp.sum(jnp.where(hit, ((lanes8 & 31) + 1).astype(F32), 0.0), axis=1, keepdims=True)
        zlist = jnp.where(lanes8 == c, code, zlist)

    right = jnp.where(ci >= 0.0, (lane + 1).astype(F32), 0.0)
    again = jnp.where(plain, float(PLAIN), right)
    again = jnp.where(((lane & 31) == p) & (ci >= 0.0), (OWN + (lane >> 5)).astype(F32), again)
    stack = jnp.where(row128 == 0, ci, jnp.where(row128 == 1, cj, jnp.where(row128 == 2, right, again))).T
    ci_c, cj_c = stack[:, 0:1], stack[:, 1:2]
    met_c = ci_c == lk
    linked = (jnp.where(met_c, stack[:, 2:3], 0.0), jnp.where(met_c, stack[:, 3:4], 0.0))
    meets = [jnp.zeros((8, 128), F32), jnp.zeros((8, 128), F32)]
    terms = jnp.zeros((8, 128), F32)
    for o in range(SLOTS):
        out_i, out_j = blocks[0, o].astype(F32), blocks[1, o].astype(F32)
        for n in range(2):
            met = jnp.sum(jnp.where(cj_c == out_j, linked[n], 0.0), axis=0, keepdims=True)
            meets[n] = jnp.where(rows8 == o, jnp.where(li == out_i, met, 0.0), meets[n])
        hit = plain & (ci == out_j) & ((lane & 31) != p)
        code = jnp.sum(jnp.where(hit, (lane + 1).astype(F32), 0.0), axis=1, keepdims=True)
        terms = jnp.where((rows8 == o) & (lanes8 == 64), code, terms)
    got_d, got_r = dl_ref[pl.ds(q, 1), :], rl_ref[pl.ds(q, 1), :]
    for t in range(LEFTS):
        if t < ZL * SLOTS:
            hit = (lane >> 5 == t // SLOTS) & (got_d > 0.5) & (got_r == float(t % SLOTS))
        else:
            hit = lane == zl * 32 + u * SLOTS + (t - ZL * SLOTS)
        for n in range(2):
            value = jnp.sum(jnp.where(hit, meets[n], 0.0), axis=1, keepdims=True)
            terms = jnp.where(lanes8 == n * 32 + t, value, terms)

    def per_dev(count):
        return dot(dot(in_row, (count * adj).astype(BF16)).astype(BF16), in_col_t)

    from_i, from_k = iota((NB, NB), 0), iota((NB, NB), 1)
    k_row = row_of(iota((1, NB), 1))
    k_col = col_of(iota((1, NB), 1))
    i_row = row_of(iota((NB, 1), 0))
    i_col = col_of(iota((NB, 1), 0))
    most = jnp.zeros((32, 32), F32)
    to_col = jnp.where(i_col != k_col, adj, 0.0).astype(BF16)
    for z in range(ZL):
        part = jnp.where((k_col >> 3) == z, adj, 0.0).astype(BF16)
        most = jnp.maximum(most, per_dev(dot(part, to_col)))
    left_over = jnp.max(most, keepdims=True) > SLOTS + 0.5
    moving = jnp.where(i_row != k_row, adj, 0.0)
    single = jnp.sum(mutual, axis=1, keepdims=True) < 1.5
    target = jnp.where((from_i == from_k) & single, 0.0, adj).astype(BF16)
    n, first, second = (
        per_dev(dot((moving * weight.astype(F32)).astype(BF16), target))
        for weight in (k_row * 0 + 1, k_row, ((k_row - 11) * (k_row - 12)) >> 1)
    )
    half = 0.5 * first
    clash = (n > 2.5) | ((n > 1.5) & ((half - 11.0) * (half - 12.0) == second))
    clash = jnp.max(jnp.where(clash, 1.0, 0.0), keepdims=True)
    level = jnp.where(left_over, 2.0, clash)
    zlist = jnp.where((rows8 == 7) & (lanes8 == 0), level, zlist)

    list_ref[0:ZLIST, :] = sends.astype(jnp.int32)
    list_ref[ZLIST:TERMS, :] = zlist.astype(jnp.int32)
    list_ref[TERMS:, :] = terms.astype(jnp.int32)
    copy = pltpu.make_async_copy(list_ref, list_smem, sem)
    copy.start()
    copy.wait()
    for d in range(ZL):
        for c in range(SLOTS):
            code = list_smem[ZLIST + d, c]

            @pl.when(code > 0)
            def _():
                k = code - 1
                src_u = (k * 11) >> 5
                start = pl.multiple_of(src_u * PANEL + (k - src_u * SLOTS) * BLK, 16)
                zbuf_ref[d, c * BLK : (c + 1) * BLK, :] = second_ref[pl.ds(start, BLK), :]


def tile_at(start):
    return pl.ds(pl.multiple_of(start, 16), BLK)


def left_at(t, left_ref, own_ref):
    if t < ZL * SLOTS:
        return left_ref.at[t * BLK : (t + 1) * BLK, :]
    t -= ZL * SLOTS
    return own_ref.at[t * BLK : (t + 1) * BLK, :]


def panel_start(code):
    r = code - 1
    return ((r & 7) * ZH + ((r >> 3) & 3)) * PANEL + (r >> 5) * BLK


def square_kernel(lists, own_ref, left_ref, right_ref, out_ref, acc_ref):
    for o in range(SLOTS):
        part = slice(o * BLK, (o + 1) * BLK)
        acc_ref[...] = jnp.zeros((BLK, BLK), F32)
        for t in range(LEFTS):
            code = lists[TERMS + o, t]
            left = left_at(t, left_ref, own_ref)

            @pl.when(code > 0)
            def _():
                acc_ref[...] += dot(left[...], right_ref[tile_at(panel_start(code)), :])

        out_ref[part, :] = acc_ref[...].astype(BF16)
        code = lists[TERMS + o, 64]

        @pl.when(code > 0)
        def _():
            tile = right_ref[tile_at(panel_start(code)), :]
            out_ref[TILES + o * BLK : TILES + (o + 1) * BLK, :] = dot(tile, tile).astype(BF16)


def send_kernel(lists, square_ref, send_ref):
    for d in range(N_ROW):
        code = lists[d, 0]

        @pl.when((code > 0) & (code <= SLOTS))
        def _():
            send_ref[d] = square_ref[tile_at((code - 1) * BLK), :]


def cube_kernel(room, lists, blocks, own_ref, left_ref, square_ref, right_ref, out_ref, level_ref, acc_ref):
    for o in range(SLOTS):
        part = slice(o * BLK, (o + 1) * BLK)
        acc_ref[...] = jnp.zeros((BLK, BLK), F32)
        for t in range(LEFTS):
            code = lists[TERMS + o, 32 + t]
            left = left_at(t, left_ref, own_ref)

            @pl.when((code > 0) & (code < OWN))
            def _():
                r = code - 1
                start = (r & 31) * BLK if room == 1 else ((r & 31) * SLOTS + (r >> 5)) * BLK
                acc_ref[...] += dot(left[...], right_ref[tile_at(start), :])

            @pl.when((code >= OWN) & (code < PLAIN))
            def _():
                acc_ref[...] += dot(left[...], square_ref[tile_at((code - OWN) * BLK), :])

            @pl.when(code == PLAIN)
            def _():
                acc_ref[...] += dot(left[...], square_ref[TILES + o * BLK : TILES + (o + 1) * BLK, :])

        value = 1.5 * own_ref[part, :].astype(F32) - 0.5 * acc_ref[...]
        out_ref[:, part] = jnp.where(blocks[0, o] >= 0, value, 0.0).astype(BF16)
    level_ref[0] = lists[TERMS - 1, 0]


def swap(value, axes):
    return lax.all_to_all(value, axes, 0, 0, tiled=True)


def like(*shape, dtype=BF16):
    return jax.ShapeDtypeStruct(shape, dtype)


def per_device(x, blocks):
    first, own = pl.pallas_call(
        pack_kernel,
        out_shape=(like(ZH, PANEL, BLK), like(TILES, BLK)),
        in_specs=[SMEM, VMEM], out_specs=(VMEM, VMEM), compiler_params=PARAMS, name="pack",
    )(blocks, x)
    first = swap(first, "zh")
    right = lax.all_gather(first.reshape(ZH * PANEL, BLK), "y", axis=0, tiled=True)
    heads = jnp.sum(first[:, TILES:].astype(F32), axis=0).astype(BF16)
    second = lax.all_gather(jnp.concatenate([own, heads], axis=0), ("x", "c"), axis=0)
    heads = jnp.sum(second[:, TILES:].astype(F32), axis=0).astype(BF16)
    heads = jnp.broadcast_to(heads[None], (Y * ZL, HEAD, 128)).reshape(Y * ZL * HEAD, 128)
    heads = swap(heads, ("y", "zl")).reshape(Y, ZL * HEAD, 128)
    zbuf, lists = pl.pallas_call(
        plan_kernel,
        out_shape=(like(ZL, TILES, BLK), like(TERMS + 8, 128, dtype=jnp.int32)),
        in_specs=[SMEM, VMEM, VMEM], out_specs=(VMEM, VMEM),
        scratch_shapes=[
            pltpu.VMEM((128, 128), F32), pltpu.VMEM((128, 128), F32),
            pltpu.VMEM((NB, SLOTS_ROW * 128), BF16), pltpu.VMEM((SLOTS_ROW * 128, NB), BF16),
            pltpu.VMEM((32, 128), F32), pltpu.VMEM((32, 128), F32),
            pltpu.SMEM((TERMS + 8, 128), jnp.int32), pltpu.SemaphoreType.DMA,
        ],
        compiler_params=PARAMS, name="plan",
    )(blocks, heads, second.reshape(XC * PANEL, BLK))
    left = swap(zbuf, "zl").reshape(ZL * TILES, BLK)
    square = pl.pallas_call(
        square_kernel,
        out_shape=like(2 * TILES, BLK),
        in_specs=[SMEM] + [VMEM] * 3, out_specs=VMEM,
        scratch_shapes=[pltpu.VMEM((BLK, BLK), F32)], compiler_params=PARAMS, name="square",
    )(lists, own, left, right)
    send = pl.pallas_call(
        send_kernel,
        out_shape=like(N_ROW, BLK, BLK),
        in_specs=[SMEM, VMEM], out_specs=VMEM, compiler_params=PARAMS, name="send",
    )(lists, square)

    def finish(room, squares, lists, blocks, own, left, square):
        return pl.pallas_call(
            lambda *refs: cube_kernel(room, *refs),
            out_shape=(like(*x.shape), like(1, dtype=jnp.int32)),
            in_specs=[SMEM, SMEM] + [VMEM] * 4, out_specs=(VMEM, SMEM),
            scratch_shapes=[pltpu.VMEM((BLK, BLK), F32)], compiler_params=PARAMS, name="cube%d" % room,
        )(lists, blocks, own, left, square, squares)


    kept = (lists, blocks, own, left, square)
    result, level = finish(1, swap(send, ROW).reshape(N_ROW * BLK, BLK), *kept)
    result, level, x, kept = lax.optimization_barrier((result, level, x, kept))

    def roomy():
        return finish(SLOTS, swap(jnp.tile(kept[-1][:TILES], (N_ROW, 1)), ROW), *kept)[0]

    return lax.switch(level[0], [lambda: result, roomy, lambda: general(x, kept[1])])


def solution(mesh):
    fine = Mesh(mesh.devices.reshape(ZH, Y, ZL, X, C), ROW + COL)
    return jax.shard_map(
        per_device,
        mesh=fine,
        in_specs=(P(ROW, COL), P(ROW, COL)),
        out_specs=P(ROW, COL),
        check_vma=False,
    )
```

```python
import jax
import jax.numpy as jnp
from jax import lax
from jax.experimental import pallas as pl
from jax.experimental.pallas import tpu as pltpu
from jax.sharding import Mesh, PartitionSpec as P

BLK = 128
NB = 384
ZH, Y, ZL, X, C = 3, 8, 4, 4, 2
XC = X * C
N_ROW, N_COL = ZH * Y, ZL * XC
SLOTS = 3
TILES = SLOTS * BLK
HEAD = 16
PANEL = TILES + HEAD
SLOTS_ROW = XC * SLOTS
LEFTS = ZL * SLOTS + SLOTS
OWN, PLAIN = 128, 160
ROOM = 2
ZLIST, TERMS = 8, 16
ROW = ("zh", "y")
COL = ("zl", "x", "c")
F32 = jnp.float32
BF16 = jnp.bfloat16
PARAMS = pltpu.CompilerParams(vmem_limit_bytes=48 * 1024 * 1024)
VMEM = pl.BlockSpec(memory_space=pltpu.VMEM)
SMEM = pl.BlockSpec(memory_space=pltpu.SMEM)


def partner(fold_rows, fold_cols, keep_rows, keep_cols, out_rows, out_cols):
    folded_r = fold_rows[:, None, None]
    folded_c = fold_cols[:, None, None]
    kept_r = keep_rows[None, None, :]
    kept_c = keep_cols[None, None, :]
    target_r = out_rows[None, :, None]
    target_c = out_cols[None, :, None]
    linked = (folded_r == target_r) & (folded_c == kept_r) & (kept_c == target_c)
    linked = linked & (folded_r >= 0) & (kept_r >= 0) & (target_r >= 0)
    positions = jnp.arange(keep_rows.shape[0], dtype=jnp.int32)[None, None, :]
    partner_slot = jnp.sum(jnp.where(linked, positions, 0), axis=2)
    return (partner_slot, jnp.any(linked, axis=2))


def columns(tile_array, tile_blocks):
    return (
        lax.all_gather(tile_array, ROW, axis=0, tiled=True),
        lax.all_gather(tile_blocks, ROW, axis=0, tiled=True),
    )


def left_fold(left_tiles, tile_blocks, panel, panel_blocks):
    block_size = left_tiles.shape[0]
    slot_count = tile_blocks.shape[1]
    panel_rows = panel.shape[0] // block_size
    right_grid = panel.reshape(panel_rows, block_size, slot_count, block_size)
    kept_blocks = panel_blocks.reshape(panel_rows, 2, slot_count)
    kept_rows = kept_blocks[:, 0].reshape(-1)
    kept_cols = kept_blocks[:, 1].reshape(-1)
    piece_tiles = lax.all_gather(left_tiles, COL, axis=1, tiled=True)
    piece_blocks = lax.all_gather(tile_blocks, COL, axis=1, tiled=True)
    piece_slots = piece_blocks.shape[1]
    left_list = piece_tiles.reshape(block_size, piece_slots, block_size)
    partner_slot, matched = partner(
        piece_blocks[0], piece_blocks[1], kept_rows, kept_cols, tile_blocks[0], tile_blocks[1]
    )
    picked = right_grid[partner_slot // slot_count, :, partner_slot % slot_count, :]
    picked = picked * matched[:, :, None, None].astype(BF16)
    running = jnp.einsum("iak,aokj->ioj", left_list, picked, preferred_element_type=F32)
    return running.reshape(block_size, slot_count * block_size)


def general(iterate_tiles, tile_blocks):
    block_size = iterate_tiles.shape[0]
    slot_count = tile_blocks.shape[1]
    panel, panel_blocks = columns(iterate_tiles, tile_blocks)
    square = left_fold(iterate_tiles, tile_blocks, panel, panel_blocks).astype(BF16)
    panel, panel_blocks = columns(square, tile_blocks)
    cube = left_fold(iterate_tiles, tile_blocks, panel, panel_blocks)
    used = tile_blocks[0] >= 0
    updated = 1.5 * iterate_tiles.astype(F32) - 0.5 * cube
    shaped = updated.reshape(block_size, slot_count, block_size)
    kept = jnp.where(used[None, :, None], shaped, jnp.zeros_like(shaped))
    return kept.reshape(block_size, slot_count * block_size).astype(BF16)


def place():
    zh, y, zl = lax.axis_index("zh"), lax.axis_index("y"), lax.axis_index("zl")
    u = lax.axis_index("x") * C + lax.axis_index("c")
    return zh, y, zl, u, zh * Y + y, zl * XC + u


def iota(shape, dim):
    return lax.broadcasted_iota(jnp.int32, shape, dim)


def dot(a, b):
    return jnp.dot(a, b, preferred_element_type=F32)


def onehot(mask):
    return jnp.where(mask, 1.0, 0.0).astype(BF16)


def row_of(number):
    return number - N_ROW * ((number * 683) >> 14)


def col_of(number):
    return (number + ((number * 683) >> 14)) & (N_COL - 1)


def pack_kernel(blocks, x_ref, out_ref, own_ref):
    zh, y, zl, u, p, q = place()
    lane = iota((HEAD, 128), 1)
    here = iota((HEAD, 128), 0) == zh
    head = jnp.zeros((HEAD, 128), F32)
    for s in range(SLOTS):
        for v in range(4):
            number = blocks[v // 2, s]
            part = (number >> 4) if v % 2 == 0 else (number & 15)
            head = jnp.where(here & (lane == v * 32 + u * SLOTS + s), part.astype(F32), head)
    head = head.astype(BF16)
    for s in range(SLOTS):
        tile = x_ref[:, s * BLK : (s + 1) * BLK]
        own_ref[s * BLK : (s + 1) * BLK, :] = tile
        for z in range(ZH):
            out_ref[z, s * BLK : (s + 1) * BLK, :] = tile
    for z in range(ZH):
        out_ref[z, TILES:, :] = head


def plan_kernel(
    blocks, g_ref, second_ref, zbuf_ref, list_ref,
    gij_ref, gt_ref, ohi_ref, ohj_ref, dy_ref, ry_ref, dl_ref, rl_ref, list_smem, sem,
):
    zh, y, zl, u, p, q = place()
    told = g_ref[...].astype(F32)
    for z in range(ZL):
        for h in range(ZH):
            gij_ref[z * 32 + h * Y : z * 32 + (h + 1) * Y, :] = told[:, z * HEAD + h, :]
        gij_ref[z * 32 + N_ROW : (z + 1) * 32, :] = jnp.zeros((32 - N_ROW, 128), F32)
    g = gij_ref[...]
    g = 16.0 * g + pltpu.roll(g, 96, 1)
    row128, lane128 = iota((128, 128), 0), iota((128, 128), 1)
    g = jnp.where(((row128 & 31) < N_ROW) & ((lane128 & 63) < SLOTS_ROW), g, -1.0)
    gij_ref[...] = g
    gt = g.T
    gt_ref[...] = gt
    sub = iota((NB, 128), 0).astype(F32)
    wide = iota((128, NB), 1).astype(F32)
    for k in range(SLOTS_ROW):
        ohi_ref[:, k * 128 : (k + 1) * 128] = onehot(sub == gt[k : k + 1, :])
        ohj_ref[k * 128 : (k + 1) * 128, :] = onehot(wide == g[:, 64 + k : 65 + k])
    adj = dot(ohi_ref[...], ohj_ref[...])
    adj_b = adj.astype(BF16)
    adj_tf = adj.T
    adj_t = adj_tf.astype(BF16)
    mutual = adj * adj_tf
    lane = iota((1, 128), 1)
    rows = iota((32, 128), 0)
    lanes = iota((32, 128), 1)
    number = iota((32, NB), 1)
    in_row = onehot(row_of(number) == iota((32, NB), 0))
    in_col = onehot(col_of(number) == iota((32, NB), 0))
    in_col_t = onehot(col_of(iota((NB, 32), 0)) == iota((NB, 32), 1))

    ci = jnp.full((1, 128), -1.0, F32)
    cj = jnp.full((1, 128), -1.0, F32)
    for s in range(SLOTS):
        shift = (s * 32 + 128 - zl * 32) & 127
        here = (lane >> 5 == s) & ((lane & 31) < N_ROW)
        rows_i = jnp.broadcast_to(gt_ref[pl.ds(u * SLOTS + s, 1), :], (8, 128))
        rows_j = jnp.broadcast_to(gt_ref[pl.ds(64 + u * SLOTS + s, 1), :], (8, 128))
        ci = jnp.where(here, pltpu.roll(rows_i, shift, 1)[0:1], ci)
        cj = jnp.where(here, pltpu.roll(rows_j, shift, 1)[0:1], cj)
    of_i = onehot(sub == ci)
    both = dot(adj_b, onehot(sub == cj)) * dot(adj_b, of_i)
    pairs = jnp.broadcast_to(jnp.sum(mutual, axis=0, keepdims=True), (8, NB)).astype(BF16)
    plain = (ci == cj) & (ci >= 0.0) & (dot(pairs, of_i)[0:1] < 1.5)
    plain_f = jnp.where(plain, 1.0, 0.0)
    wanted = (dot(in_row, both.astype(BF16)) > 0.5) & ((lanes & 31) != rows) & (plain_f < 0.5)
    wanted = jnp.where(wanted, 1.0, 0.0)
    dy_ref[...] = wanted
    ry_ref[...] = dot(wanted.astype(BF16), onehot((row128 < lane128) & ((row128 & 7) == (lane128 & 7))))
    lanes8 = iota((8, 128), 1)
    rows8 = iota((8, 128), 0)
    send_d = dy_ref[pl.ds(pl.multiple_of(zh * Y, 8), 8), :]
    send_r = ry_ref[pl.ds(pl.multiple_of(zh * Y, 8), 8), :]
    ylist = jnp.zeros((8, 128), F32)
    for c in range(ROOM):
        hit = (send_d > 0.5) & (send_r == float(c)) & ((lanes8 & 7) == y)
        code = jnp.sum(jnp.where(hit, (lanes8 + 1).astype(F32), 0.0), axis=1, keepdims=True)
        ylist = jnp.where(lanes8 == c, code, ylist)

    li = jnp.full((1, 128), -1.0, F32)
    lk = jnp.full((1, 128), -1.0, F32)
    for z in range(ZL):
        here = (lane >> 5 == z) & ((lane & 31) < SLOTS_ROW)
        mine = jnp.broadcast_to(gij_ref[pl.ds(z * 32 + p, 1), :], (8, 128))
        li = jnp.where(here, (pltpu.roll(mine, z * 32, 1) if z else mine)[0:1], li)
        lk = jnp.where(here, pltpu.roll(mine, (64 + z * 32) % 128, 1)[0:1], lk)
    both = dot(adj_t, onehot(sub == li)) * dot(adj_t, onehot(sub == lk))
    owner = (lanes >> 5) * XC + (((lanes & 31) * 11) >> 5)
    wanted = (dot(in_col, both.astype(BF16)) > 0.5) & (owner != rows) & ((lanes & 31) < SLOTS_ROW)
    wanted = jnp.where(wanted, 1.0, 0.0)
    dl_ref[...] = wanted
    rl_ref[...] = dot(wanted.astype(BF16), onehot((row128 < lane128) & ((row128 >> 5) == (lane128 >> 5))))
    send_d = jnp.zeros((8, 128), F32)
    send_r = jnp.zeros((8, 128), F32)
    for z in range(ZL):
        send_d = jnp.where(rows8 == z, dl_ref[pl.ds(z * XC + u, 1), :], send_d)
        send_r = jnp.where(rows8 == z, rl_ref[pl.ds(z * XC + u, 1), :], send_r)
    zlist = jnp.zeros((8, 128), F32)
    for c in range(SLOTS):
        hit = (send_d > 0.5) & (send_r == float(c)) & ((lanes8 >> 5) == zl)
        code = jnp.sum(jnp.where(hit, ((lanes8 & 31) + 1).astype(F32), 0.0), axis=1, keepdims=True)
        zlist = jnp.where(lanes8 == c, code, zlist)

    right = jnp.where(ci >= 0.0, (lane + 1).astype(F32), 0.0)
    got_d, got_r = dy_ref[pl.ds(p, 1), :], ry_ref[pl.ds(p, 1), :]
    again = jnp.where(got_d > 0.5, ((lane & 7) * ROOM + 1).astype(F32) + got_r, 0.0)
    again = jnp.where(plain, float(PLAIN), again)
    again = jnp.where(((lane & 31) == p) & (ci >= 0.0), (OWN + (lane >> 5)).astype(F32), again)
    stack = jnp.where(row128 == 0, ci, jnp.where(row128 == 1, cj, jnp.where(row128 == 2, right, again))).T
    ci_c, cj_c = stack[:, 0:1], stack[:, 1:2]
    met_c = ci_c == lk
    linked = (jnp.where(met_c, stack[:, 2:3], 0.0), jnp.where(met_c, stack[:, 3:4], 0.0))
    meets = [jnp.zeros((8, 128), F32), jnp.zeros((8, 128), F32)]
    terms = jnp.zeros((8, 128), F32)
    for o in range(SLOTS):
        out_i, out_j = blocks[0, o].astype(F32), blocks[1, o].astype(F32)
        for n in range(2):
            met = jnp.sum(jnp.where(cj_c == out_j, linked[n], 0.0), axis=0, keepdims=True)
            meets[n] = jnp.where(rows8 == o, jnp.where(li == out_i, met, 0.0), meets[n])
        hit = plain & (ci == out_j) & ((lane & 31) != p)
        code = jnp.sum(jnp.where(hit, (lane + 1).astype(F32), 0.0), axis=1, keepdims=True)
        terms = jnp.where((rows8 == o) & (lanes8 == 64), code, terms)
    got_d, got_r = dl_ref[pl.ds(q, 1), :], rl_ref[pl.ds(q, 1), :]
    for t in range(LEFTS):
        if t < ZL * SLOTS:
            hit = (lane >> 5 == t // SLOTS) & (got_d > 0.5) & (got_r == float(t % SLOTS))
        else:
            hit = lane == zl * 32 + u * SLOTS + (t - ZL * SLOTS)
        for n in range(2):
            value = jnp.sum(jnp.where(hit, meets[n], 0.0), axis=1, keepdims=True)
            terms = jnp.where(lanes8 == n * 32 + t, value, terms)

    def per_dev(count):
        return dot(dot(in_row, (count * adj).astype(BF16)).astype(BF16), in_col_t)

    from_i, from_k = iota((NB, NB), 0), iota((NB, NB), 1)
    k_row = row_of(iota((1, NB), 1))
    k_col = col_of(iota((1, NB), 1))
    i_row = row_of(iota((NB, 1), 0))
    i_col = col_of(iota((NB, 1), 0))
    def fullest(total, parts, room):
        least = total
        for part in parts:
            least = jnp.minimum(least, jnp.maximum(part, total - part))
        return jnp.max(jnp.where(least > room + 0.5, 1.0, 0.0), keepdims=True)

    to_col = jnp.where(i_col != k_col, adj, 0.0).astype(BF16)
    total = per_dev(dot(adj_b, to_col))
    parts = [
        per_dev(dot(jnp.where(((k_col >> bit) & 1) == 1, adj, 0.0).astype(BF16), to_col)) for bit in (3, 4)
    ]
    over = fullest(total, parts, SLOTS)
    moving = jnp.where(i_row != k_row, adj, 0.0)
    single = jnp.sum(mutual, axis=1, keepdims=True) < 1.5
    target = jnp.where((from_i == from_k) & single, 0.0, adj).astype(BF16)
    total = per_dev(dot(moving.astype(BF16), target))
    parts = [
        per_dev(dot(jnp.where(((k_row >> bit) & 1) == 1, moving, 0.0).astype(BF16), target)) for bit in (0, 1, 2)
    ]
    over = jnp.maximum(over, fullest(total, parts, ROOM))
    zlist = jnp.where((rows8 == 7) & (lanes8 == 0), over, zlist)

    list_ref[0:ZLIST, :] = ylist.astype(jnp.int32)
    list_ref[ZLIST:TERMS, :] = zlist.astype(jnp.int32)
    list_ref[TERMS:, :] = terms.astype(jnp.int32)
    copy = pltpu.make_async_copy(list_ref, list_smem, sem)
    copy.start()
    copy.wait()
    for d in range(ZL):
        for c in range(SLOTS):
            code = list_smem[ZLIST + d, c]

            @pl.when(code > 0)
            def _():
                k = code - 1
                src_u = (k * 11) >> 5
                start = pl.multiple_of(src_u * PANEL + (k - src_u * SLOTS) * BLK, 16)
                zbuf_ref[d, c * BLK : (c + 1) * BLK, :] = second_ref[pl.ds(start, BLK), :]


def tile_at(start):
    return pl.ds(pl.multiple_of(start, 16), BLK)


def left_at(t, left_ref, own_ref):
    if t < ZL * SLOTS:
        return left_ref.at[t * BLK : (t + 1) * BLK, :]
    t -= ZL * SLOTS
    return own_ref.at[t * BLK : (t + 1) * BLK, :]


def panel_start(code):
    r = code - 1
    return ((r & 7) * ZH + ((r >> 3) & 3)) * PANEL + (r >> 5) * BLK


def square_kernel(lists, own_ref, left_ref, right_ref, out_ref, near_ref, acc_ref):
    for o in range(SLOTS):
        part = slice(o * BLK, (o + 1) * BLK)
        acc_ref[...] = jnp.zeros((BLK, BLK), F32)
        for t in range(LEFTS):
            code = lists[TERMS + o, t]
            left = left_at(t, left_ref, own_ref)

            @pl.when(code > 0)
            def _():
                acc_ref[...] += dot(left[...], right_ref[tile_at(panel_start(code)), :])

        tile = acc_ref[...].astype(BF16)
        near_ref[part, :] = tile
        for z in range(ZH):
            out_ref[z, part, :] = tile
        code = lists[TERMS + o, 64]

        @pl.when(code > 0)
        def _():
            tile = right_ref[tile_at(panel_start(code)), :]
            near_ref[TILES + o * BLK : TILES + (o + 1) * BLK, :] = dot(tile, tile).astype(BF16)


def send_kernel(lists, square_ref, send_ref):
    for d in range(Y):
        for c in range(ROOM):
            code = lists[d, c]

            @pl.when(code > 0)
            def _():
                r = code - 1
                start = ((r >> 3) & 3) * TILES + (r >> 5) * BLK
                send_ref[d, c * BLK : (c + 1) * BLK, :] = square_ref[tile_at(start), :]


def cube_kernel(lists, blocks, own_ref, left_ref, near_ref, right_ref, out_ref, level_ref, acc_ref):
    for o in range(SLOTS):
        part = slice(o * BLK, (o + 1) * BLK)
        acc_ref[...] = jnp.zeros((BLK, BLK), F32)
        for t in range(LEFTS):
            code = lists[TERMS + o, 32 + t]
            left = left_at(t, left_ref, own_ref)

            @pl.when((code > 0) & (code <= Y * ROOM))
            def _():
                acc_ref[...] += dot(left[...], right_ref[tile_at((code - 1) * BLK), :])

            @pl.when(code >= OWN)
            def _():
                start = jnp.where(code == PLAIN, TILES + o * BLK, (code - OWN) * BLK)
                acc_ref[...] += dot(left[...], near_ref[tile_at(start), :])

        value = 1.5 * own_ref[part, :].astype(F32) - 0.5 * acc_ref[...]
        out_ref[:, part] = jnp.where(blocks[0, o] >= 0, value, 0.0).astype(BF16)
    level_ref[0] = lists[TERMS - 1, 0]


def swap(value, axes):
    return lax.all_to_all(value, axes, 0, 0, tiled=True)


def like(*shape, dtype=BF16):
    return jax.ShapeDtypeStruct(shape, dtype)


def per_device(x, blocks):
    first, own = pl.pallas_call(
        pack_kernel,
        out_shape=(like(ZH, PANEL, BLK), like(TILES, BLK)),
        in_specs=[SMEM, VMEM], out_specs=(VMEM, VMEM), compiler_params=PARAMS, name="pack",
    )(blocks, x)
    first = swap(first, "zh")
    right = lax.all_gather(first.reshape(ZH * PANEL, BLK), "y", axis=0, tiled=True)
    heads = jnp.sum(first[:, TILES:].astype(F32), axis=0).astype(BF16)
    second = lax.all_gather(jnp.concatenate([own, heads], axis=0), ("x", "c"), axis=0)
    heads = jnp.sum(second[:, TILES:].astype(F32), axis=0).astype(BF16)
    heads = jnp.broadcast_to(heads[None], (Y * ZL, HEAD, 128)).reshape(Y * ZL * HEAD, 128)
    heads = swap(heads, ("y", "zl")).reshape(Y, ZL * HEAD, 128)
    zbuf, lists = pl.pallas_call(
        plan_kernel,
        out_shape=(like(ZL, TILES, BLK), like(TERMS + 8, 128, dtype=jnp.int32)),
        in_specs=[SMEM, VMEM, VMEM], out_specs=(VMEM, VMEM),
        scratch_shapes=[
            pltpu.VMEM((128, 128), F32), pltpu.VMEM((128, 128), F32),
            pltpu.VMEM((NB, SLOTS_ROW * 128), BF16), pltpu.VMEM((SLOTS_ROW * 128, NB), BF16),
            pltpu.VMEM((32, 128), F32), pltpu.VMEM((32, 128), F32),
            pltpu.VMEM((32, 128), F32), pltpu.VMEM((32, 128), F32),
            pltpu.SMEM((TERMS + 8, 128), jnp.int32), pltpu.SemaphoreType.DMA,
        ],
        compiler_params=PARAMS, name="plan",
    )(blocks, heads, second.reshape(XC * PANEL, BLK))
    left = swap(zbuf, "zl").reshape(ZL * TILES, BLK)
    square, near = pl.pallas_call(
        square_kernel,
        out_shape=(like(ZH, TILES, BLK), like(2 * TILES, BLK)),
        in_specs=[SMEM] + [VMEM] * 3, out_specs=(VMEM, VMEM),
        scratch_shapes=[pltpu.VMEM((BLK, BLK), F32)], compiler_params=PARAMS, name="square",
    )(lists, own, left, right)
    square = swap(square, "zh").reshape(ZH * TILES, BLK)
    send = pl.pallas_call(
        send_kernel,
        out_shape=like(Y, ROOM * BLK, BLK),
        in_specs=[SMEM, VMEM], out_specs=VMEM, compiler_params=PARAMS, name="send",
    )(lists, square)
    result, level = pl.pallas_call(
        cube_kernel,
        out_shape=(like(*x.shape), like(1, dtype=jnp.int32)),
        in_specs=[SMEM, SMEM] + [VMEM] * 4, out_specs=(VMEM, SMEM),
        scratch_shapes=[pltpu.VMEM((BLK, BLK), F32)], compiler_params=PARAMS, name="cube",
    )(lists, blocks, own, left, near, swap(send, "y").reshape(Y * ROOM * BLK, BLK))
    result, level, x, blocks = lax.optimization_barrier((result, level, x, blocks))
    return lax.cond(level[0] > 0, lambda: general(x, blocks), lambda: result)


def solution(mesh):
    fine = Mesh(mesh.devices.reshape(ZH, Y, ZL, X, C), ROW + COL)
    return jax.shard_map(
        per_device,
        mesh=fine,
        in_specs=(P(ROW, COL), P(ROW, COL)),
        out_specs=P(ROW, COL),
        check_vma=False,
    )
```

```python
import jax
import jax.numpy as jnp
from jax import lax
from jax.experimental import pallas as pl
from jax.experimental.pallas import tpu as pltpu
from jax.sharding import Mesh, PartitionSpec as P

BLK = 128
NB = 384
ZH, Y, ZL, X, C = 3, 8, 4, 4, 2
XC = X * C
N_ROW, N_COL = ZH * Y, ZL * XC
SLOTS = 3
TILES = SLOTS * BLK
HEAD = 16
PANEL = TILES + HEAD
SLOTS_ROW = XC * SLOTS
LEFTS = ZL * SLOTS + SLOTS
OWN, PLAIN = 128, 160
ROOM = 2
ZLIST, TERMS = 8, 16
ROW = ("zh", "y")
COL = ("zl", "x", "c")
F32 = jnp.float32
BF16 = jnp.bfloat16
PARAMS = pltpu.CompilerParams(vmem_limit_bytes=48 * 1024 * 1024)
VMEM = pl.BlockSpec(memory_space=pltpu.VMEM)
SMEM = pl.BlockSpec(memory_space=pltpu.SMEM)


def partner(fold_rows, fold_cols, keep_rows, keep_cols, out_rows, out_cols):
    folded_r = fold_rows[:, None, None]
    folded_c = fold_cols[:, None, None]
    kept_r = keep_rows[None, None, :]
    kept_c = keep_cols[None, None, :]
    target_r = out_rows[None, :, None]
    target_c = out_cols[None, :, None]
    linked = (folded_r == target_r) & (folded_c == kept_r) & (kept_c == target_c)
    linked = linked & (folded_r >= 0) & (kept_r >= 0) & (target_r >= 0)
    positions = jnp.arange(keep_rows.shape[0], dtype=jnp.int32)[None, None, :]
    partner_slot = jnp.sum(jnp.where(linked, positions, 0), axis=2)
    return (partner_slot, jnp.any(linked, axis=2))


def columns(tile_array, tile_blocks):
    return (
        lax.all_gather(tile_array, ROW, axis=0, tiled=True),
        lax.all_gather(tile_blocks, ROW, axis=0, tiled=True),
    )


def left_fold(left_tiles, tile_blocks, panel, panel_blocks):
    block_size = left_tiles.shape[0]
    slot_count = tile_blocks.shape[1]
    panel_rows = panel.shape[0] // block_size
    right_grid = panel.reshape(panel_rows, block_size, slot_count, block_size)
    kept_blocks = panel_blocks.reshape(panel_rows, 2, slot_count)
    kept_rows = kept_blocks[:, 0].reshape(-1)
    kept_cols = kept_blocks[:, 1].reshape(-1)
    piece_tiles = lax.all_gather(left_tiles, COL, axis=1, tiled=True)
    piece_blocks = lax.all_gather(tile_blocks, COL, axis=1, tiled=True)
    piece_slots = piece_blocks.shape[1]
    left_list = piece_tiles.reshape(block_size, piece_slots, block_size)
    partner_slot, matched = partner(
        piece_blocks[0], piece_blocks[1], kept_rows, kept_cols, tile_blocks[0], tile_blocks[1]
    )
    picked = right_grid[partner_slot // slot_count, :, partner_slot % slot_count, :]
    picked = picked * matched[:, :, None, None].astype(BF16)
    running = jnp.einsum("iak,aokj->ioj", left_list, picked, preferred_element_type=F32)
    return running.reshape(block_size, slot_count * block_size)


def general(iterate_tiles, tile_blocks):
    block_size = iterate_tiles.shape[0]
    slot_count = tile_blocks.shape[1]
    panel, panel_blocks = columns(iterate_tiles, tile_blocks)
    square = left_fold(iterate_tiles, tile_blocks, panel, panel_blocks).astype(BF16)
    panel, panel_blocks = columns(square, tile_blocks)
    cube = left_fold(iterate_tiles, tile_blocks, panel, panel_blocks)
    used = tile_blocks[0] >= 0
    updated = 1.5 * iterate_tiles.astype(F32) - 0.5 * cube
    shaped = updated.reshape(block_size, slot_count, block_size)
    kept = jnp.where(used[None, :, None], shaped, jnp.zeros_like(shaped))
    return kept.reshape(block_size, slot_count * block_size).astype(BF16)


def place():
    zh, y, zl = lax.axis_index("zh"), lax.axis_index("y"), lax.axis_index("zl")
    u = lax.axis_index("x") * C + lax.axis_index("c")
    return zh, y, zl, u, zh * Y + y, zl * XC + u


def iota(shape, dim):
    return lax.broadcasted_iota(jnp.int32, shape, dim)


def dot(a, b):
    return jnp.dot(a, b, preferred_element_type=F32)


def onehot(mask):
    return jnp.where(mask, 1.0, 0.0).astype(BF16)


def row_of(number):
    return number - N_ROW * ((number * 683) >> 14)


def col_of(number):
    return (number + ((number * 683) >> 14)) & (N_COL - 1)


def pack_kernel(blocks, x_ref, out_ref, own_ref):
    zh, y, zl, u, p, q = place()
    lane = iota((HEAD, 128), 1)
    here = iota((HEAD, 128), 0) == zh
    head = jnp.zeros((HEAD, 128), F32)
    for s in range(SLOTS):
        for v in range(4):
            number = blocks[v // 2, s]
            part = (number >> 4) if v % 2 == 0 else (number & 15)
            head = jnp.where(here & (lane == v * 32 + u * SLOTS + s), part.astype(F32), head)
    head = head.astype(BF16)
    for s in range(SLOTS):
        tile = x_ref[:, s * BLK : (s + 1) * BLK]
        own_ref[s * BLK : (s + 1) * BLK, :] = tile
        for z in range(ZH):
            out_ref[z, s * BLK : (s + 1) * BLK, :] = tile
    for z in range(ZH):
        out_ref[z, TILES:, :] = head


def row_tiles(gij_ref, p, lane):
    li = jnp.full((1, 128), -1.0, F32)
    lk = jnp.full((1, 128), -1.0, F32)
    for z in range(ZL):
        here = (lane >> 5 == z) & ((lane & 31) < SLOTS_ROW)
        mine = jnp.broadcast_to(gij_ref[pl.ds(z * 32 + p, 1), :], (8, 128))
        li = jnp.where(here, (pltpu.roll(mine, z * 32, 1) if z else mine)[0:1], li)
        lk = jnp.where(here, pltpu.roll(mine, (64 + z * 32) % 128, 1)[0:1], lk)
    return li, lk


def left_kernel(
    g_ref, second_ref, zbuf_ref, gij_ref, adj_ref, dl_ref, rl_ref,
    ohi_ref, ohj_ref, list_ref, list_smem, sem,
):
    zh, y, zl, u, p, q = place()
    told = g_ref[...].astype(F32)
    for z in range(ZL):
        for h in range(ZH):
            gij_ref[z * 32 + h * Y : z * 32 + (h + 1) * Y, :] = told[:, z * HEAD + h, :]
        gij_ref[z * 32 + N_ROW : (z + 1) * 32, :] = jnp.zeros((32 - N_ROW, 128), F32)
    g = gij_ref[...]
    g = 16.0 * g + pltpu.roll(g, 96, 1)
    row128, lane128 = iota((128, 128), 0), iota((128, 128), 1)
    g = jnp.where(((row128 & 31) < N_ROW) & ((lane128 & 63) < SLOTS_ROW), g, -1.0)
    gij_ref[...] = g
    gt = g.T
    sub = iota((NB, 128), 0).astype(F32)
    wide = iota((128, NB), 1).astype(F32)
    for k in range(SLOTS_ROW):
        ohi_ref[:, k * 128 : (k + 1) * 128] = onehot(sub == gt[k : k + 1, :])
        ohj_ref[k * 128 : (k + 1) * 128, :] = onehot(wide == g[:, 64 + k : 65 + k])
    adj_b = dot(ohi_ref[...], ohj_ref[...]).astype(BF16)
    adj_ref[...] = adj_b
    lane = iota((1, 128), 1)
    rows, lanes = iota((32, 128), 0), iota((32, 128), 1)
    rows8, lanes8 = iota((8, 128), 0), iota((8, 128), 1)
    in_col = onehot(col_of(iota((32, NB), 1)) == iota((32, NB), 0))

    li, lk = row_tiles(gij_ref, p, lane)
    stack = jnp.where(row128 == 0, li, lk).T
    both = dot(onehot(wide == stack[:, 0:1]), adj_b) * dot(onehot(wide == stack[:, 1:2]), adj_b)
    count = lax.dot_general(in_col, both.astype(BF16), (((1,), (1,)), ((), ())), preferred_element_type=F32)
    owner = (lanes >> 5) * XC + (((lanes & 31) * 11) >> 5)
    wanted = (count > 0.5) & (owner != rows) & ((lanes & 31) < SLOTS_ROW)
    wanted = jnp.where(wanted, 1.0, 0.0)
    dl_ref[...] = wanted
    rl_ref[...] = dot(wanted.astype(BF16), onehot((row128 < lane128) & ((row128 >> 5) == (lane128 >> 5))))
    send_d = jnp.zeros((8, 128), F32)
    send_r = jnp.zeros((8, 128), F32)
    for z in range(ZL):
        send_d = jnp.where(rows8 == z, dl_ref[pl.ds(z * XC + u, 1), :], send_d)
        send_r = jnp.where(rows8 == z, rl_ref[pl.ds(z * XC + u, 1), :], send_r)
    zlist = jnp.zeros((8, 128), F32)
    for c in range(SLOTS):
        hit = (send_d > 0.5) & (send_r == float(c)) & ((lanes8 >> 5) == zl)
        code = jnp.sum(jnp.where(hit, ((lanes8 & 31) + 1).astype(F32), 0.0), axis=1, keepdims=True)
        zlist = jnp.where(lanes8 == c, code, zlist)

    list_ref[...] = zlist.astype(jnp.int32)
    copy = pltpu.make_async_copy(list_ref, list_smem, sem)
    copy.start()
    copy.wait()
    for d in range(ZL):
        for c in range(SLOTS):
            code = list_smem[d, c]

            @pl.when(code > 0)
            def _():
                k = code - 1
                src_u = (k * 11) >> 5
                start = pl.multiple_of(src_u * PANEL + (k - src_u * SLOTS) * BLK, 16)
                zbuf_ref[d, c * BLK : (c + 1) * BLK, :] = second_ref[pl.ds(start, BLK), :]


def term_kernel(
    blocks, gij_ref, adj_ref, dl_ref, rl_ref, list_ref, gt_ref, dy_ref, ry_ref,
):
    zh, y, zl, u, p, q = place()
    gt_ref[...] = gij_ref[...].T
    row128, lane128 = iota((128, 128), 0), iota((128, 128), 1)
    sub = iota((NB, 128), 0).astype(F32)
    adj_b = adj_ref[...]
    adj = adj_b.astype(F32)
    mutual = adj * adj.T
    lane = iota((1, 128), 1)
    lanes = iota((32, 128), 1)
    rows = iota((32, 128), 0)
    in_row = onehot(row_of(iota((32, NB), 1)) == iota((32, NB), 0))
    in_col_t = onehot(col_of(iota((NB, 32), 0)) == iota((NB, 32), 1))

    ci = jnp.full((1, 128), -1.0, F32)
    cj = jnp.full((1, 128), -1.0, F32)
    for s in range(SLOTS):
        shift = (s * 32 + 128 - zl * 32) & 127
        here = (lane >> 5 == s) & ((lane & 31) < N_ROW)
        rows_i = jnp.broadcast_to(gt_ref[pl.ds(u * SLOTS + s, 1), :], (8, 128))
        rows_j = jnp.broadcast_to(gt_ref[pl.ds(64 + u * SLOTS + s, 1), :], (8, 128))
        ci = jnp.where(here, pltpu.roll(rows_i, shift, 1)[0:1], ci)
        cj = jnp.where(here, pltpu.roll(rows_j, shift, 1)[0:1], cj)
    of_i = onehot(sub == ci)
    both = dot(adj_b, onehot(sub == cj)) * dot(adj_b, of_i)
    pairs = jnp.broadcast_to(jnp.sum(mutual, axis=0, keepdims=True), (8, NB)).astype(BF16)
    plain = (ci == cj) & (ci >= 0.0) & (dot(pairs, of_i)[0:1] < 1.5)
    plain_f = jnp.where(plain, 1.0, 0.0)
    wanted = (dot(in_row, both.astype(BF16)) > 0.5) & ((lanes & 31) != rows) & (plain_f < 0.5)
    wanted = jnp.where(wanted, 1.0, 0.0)
    dy_ref[...] = wanted
    ry_ref[...] = dot(wanted.astype(BF16), onehot((row128 < lane128) & ((row128 & 7) == (lane128 & 7))))
    lanes8 = iota((8, 128), 1)
    rows8 = iota((8, 128), 0)
    send_d = dy_ref[pl.ds(pl.multiple_of(zh * Y, 8), 8), :]
    send_r = ry_ref[pl.ds(pl.multiple_of(zh * Y, 8), 8), :]
    ylist = jnp.zeros((8, 128), F32)
    for c in range(ROOM):
        hit = (send_d > 0.5) & (send_r == float(c)) & ((lanes8 & 7) == y)
        code = jnp.sum(jnp.where(hit, (lanes8 + 1).astype(F32), 0.0), axis=1, keepdims=True)
        ylist = jnp.where(lanes8 == c, code, ylist)

    li, lk = row_tiles(gij_ref, p, lane)

    right = jnp.where(ci >= 0.0, (lane + 1).astype(F32), 0.0)
    got_d, got_r = dy_ref[pl.ds(p, 1), :], ry_ref[pl.ds(p, 1), :]
    again = jnp.where(got_d > 0.5, ((lane & 7) * ROOM + 1).astype(F32) + got_r, 0.0)
    again = jnp.where(plain, float(PLAIN), again)
    again = jnp.where(((lane & 31) == p) & (ci >= 0.0), (OWN + (lane >> 5)).astype(F32), again)
    stack = jnp.where(row128 == 0, ci, jnp.where(row128 == 1, cj, jnp.where(row128 == 2, right, again))).T
    ci_c, cj_c = stack[:, 0:1], stack[:, 1:2]
    met_c = ci_c == lk
    linked = (jnp.where(met_c, stack[:, 2:3], 0.0), jnp.where(met_c, stack[:, 3:4], 0.0))
    meets = [jnp.zeros((8, 128), F32), jnp.zeros((8, 128), F32)]
    terms = jnp.zeros((8, 128), F32)
    for o in range(SLOTS):
        out_i, out_j = blocks[0, o].astype(F32), blocks[1, o].astype(F32)
        for n in range(2):
            met = jnp.sum(jnp.where(cj_c == out_j, linked[n], 0.0), axis=0, keepdims=True)
            meets[n] = jnp.where(rows8 == o, jnp.where(li == out_i, met, 0.0), meets[n])
        hit = plain & (ci == out_j) & ((lane & 31) != p)
        code = jnp.sum(jnp.where(hit, (lane + 1).astype(F32), 0.0), axis=1, keepdims=True)
        terms = jnp.where((rows8 == o) & (lanes8 == 64), code, terms)
    got_d, got_r = dl_ref[pl.ds(q, 1), :], rl_ref[pl.ds(q, 1), :]
    for t in range(LEFTS):
        if t < ZL * SLOTS:
            hit = (lane >> 5 == t // SLOTS) & (got_d > 0.5) & (got_r == float(t % SLOTS))
        else:
            hit = lane == zl * 32 + u * SLOTS + (t - ZL * SLOTS)
        for n in range(2):
            value = jnp.sum(jnp.where(hit, meets[n], 0.0), axis=1, keepdims=True)
            terms = jnp.where(lanes8 == n * 32 + t, value, terms)

    def per_dev(count):
        return dot(dot(in_row, (count * adj).astype(BF16)).astype(BF16), in_col_t)

    from_i, from_k = iota((NB, NB), 0), iota((NB, NB), 1)
    k_row = row_of(iota((1, NB), 1))
    k_col = col_of(iota((1, NB), 1))
    i_row = row_of(iota((NB, 1), 0))
    i_col = col_of(iota((NB, 1), 0))
    def fullest(total, parts, room):
        least = total
        for part in parts:
            least = jnp.minimum(least, jnp.maximum(part, total - part))
        return jnp.max(jnp.where(least > room + 0.5, 1.0, 0.0), keepdims=True)

    to_col = jnp.where(i_col != k_col, adj, 0.0).astype(BF16)
    total = per_dev(dot(adj_b, to_col))
    parts = [
        per_dev(dot(jnp.where(((k_col >> bit) & 1) == 1, adj, 0.0).astype(BF16), to_col)) for bit in (3, 4)
    ]
    over = fullest(total, parts, SLOTS)
    moving = jnp.where(i_row != k_row, adj, 0.0)
    single = jnp.sum(mutual, axis=1, keepdims=True) < 1.5
    target = jnp.where((from_i == from_k) & single, 0.0, adj).astype(BF16)
    total = per_dev(dot(moving.astype(BF16), target))
    parts = [
        per_dev(dot(jnp.where(((k_row >> bit) & 1) == 1, moving, 0.0).astype(BF16), target)) for bit in (0, 1, 2)
    ]
    over = jnp.maximum(over, fullest(total, parts, ROOM))
    level = jnp.where((rows8 == 7) & (lanes8 == 0), over, 0.0)

    list_ref[0:ZLIST, :] = ylist.astype(jnp.int32)
    list_ref[ZLIST:TERMS, :] = level.astype(jnp.int32)
    list_ref[TERMS:, :] = terms.astype(jnp.int32)


def tile_at(start):
    return pl.ds(pl.multiple_of(start, 16), BLK)


def left_at(t, left_ref, own_ref):
    if t < ZL * SLOTS:
        return left_ref.at[t * BLK : (t + 1) * BLK, :]
    t -= ZL * SLOTS
    return own_ref.at[t * BLK : (t + 1) * BLK, :]


def panel_start(code):
    r = code - 1
    return ((r & 7) * ZH + ((r >> 3) & 3)) * PANEL + (r >> 5) * BLK


def square_kernel(lists, own_ref, left_ref, right_ref, out_ref, near_ref, acc_ref):
    for o in range(SLOTS):
        part = slice(o * BLK, (o + 1) * BLK)
        acc_ref[...] = jnp.zeros((BLK, BLK), F32)
        for t in range(LEFTS):
            code = lists[TERMS + o, t]
            left = left_at(t, left_ref, own_ref)

            @pl.when(code > 0)
            def _():
                acc_ref[...] += dot(left[...], right_ref[tile_at(panel_start(code)), :])

        tile = acc_ref[...].astype(BF16)
        near_ref[part, :] = tile
        for z in range(ZH):
            out_ref[z, part, :] = tile
        code = lists[TERMS + o, 64]

        @pl.when(code > 0)
        def _():
            tile = right_ref[tile_at(panel_start(code)), :]
            near_ref[TILES + o * BLK : TILES + (o + 1) * BLK, :] = dot(tile, tile).astype(BF16)


def send_kernel(lists, square_ref, send_ref):
    for d in range(Y):
        for c in range(ROOM):
            code = lists[d, c]

            @pl.when(code > 0)
            def _():
                r = code - 1
                start = ((r >> 3) & 3) * TILES + (r >> 5) * BLK
                send_ref[d, c * BLK : (c + 1) * BLK, :] = square_ref[tile_at(start), :]


def cube_kernel(lists, blocks, own_ref, left_ref, near_ref, right_ref, out_ref, level_ref, acc_ref):
    for o in range(SLOTS):
        part = slice(o * BLK, (o + 1) * BLK)
        acc_ref[...] = jnp.zeros((BLK, BLK), F32)
        for t in range(LEFTS):
            code = lists[TERMS + o, 32 + t]
            left = left_at(t, left_ref, own_ref)

            @pl.when((code > 0) & (code <= Y * ROOM))
            def _():
                acc_ref[...] += dot(left[...], right_ref[tile_at((code - 1) * BLK), :])

            @pl.when(code >= OWN)
            def _():
                start = jnp.where(code == PLAIN, TILES + o * BLK, (code - OWN) * BLK)
                acc_ref[...] += dot(left[...], near_ref[tile_at(start), :])

        value = 1.5 * own_ref[part, :].astype(F32) - 0.5 * acc_ref[...]
        out_ref[:, part] = jnp.where(blocks[0, o] >= 0, value, 0.0).astype(BF16)
    level_ref[0] = lists[TERMS - 1, 0]


def swap(value, axes):
    return lax.all_to_all(value, axes, 0, 0, tiled=True)


def like(*shape, dtype=BF16):
    return jax.ShapeDtypeStruct(shape, dtype)


def per_device(x, blocks):
    first, own = pl.pallas_call(
        pack_kernel,
        out_shape=(like(ZH, PANEL, BLK), like(TILES, BLK)),
        in_specs=[SMEM, VMEM], out_specs=(VMEM, VMEM), compiler_params=PARAMS, name="pack",
    )(blocks, x)
    first = swap(first, "zh")
    right = lax.all_gather(first.reshape(ZH * PANEL, BLK), "y", axis=0, tiled=True)
    heads = jnp.sum(first[:, TILES:].astype(F32), axis=0).astype(BF16)
    second = lax.all_gather(jnp.concatenate([own, heads], axis=0), ("x", "c"), axis=0)
    heads = jnp.sum(second[:, TILES:].astype(F32), axis=0).astype(BF16)
    heads = jnp.broadcast_to(heads[None], (Y * ZL, HEAD, 128)).reshape(Y * ZL * HEAD, 128)
    heads = swap(heads, ("y", "zl")).reshape(Y, ZL * HEAD, 128)
    zbuf, known, adjacent, wanted, ranks = pl.pallas_call(
        left_kernel,
        out_shape=(
            like(ZL, TILES, BLK), like(128, 128, dtype=F32), like(NB, NB),
            like(32, 128, dtype=F32), like(32, 128, dtype=F32),
        ),
        in_specs=[VMEM, VMEM], out_specs=(VMEM,) * 5,
        scratch_shapes=[
            pltpu.VMEM((NB, SLOTS_ROW * 128), BF16), pltpu.VMEM((SLOTS_ROW * 128, NB), BF16),
            pltpu.VMEM((8, 128), jnp.int32), pltpu.SMEM((8, 128), jnp.int32), pltpu.SemaphoreType.DMA,
        ],
        compiler_params=PARAMS, name="left",
    )(heads, second.reshape(XC * PANEL, BLK))
    left = swap(zbuf, "zl").reshape(ZL * TILES, BLK)
    lists = pl.pallas_call(
        term_kernel,
        out_shape=like(TERMS + 8, 128, dtype=jnp.int32),
        in_specs=[SMEM] + [VMEM] * 4, out_specs=VMEM,
        scratch_shapes=[pltpu.VMEM((128, 128), F32), pltpu.VMEM((32, 128), F32), pltpu.VMEM((32, 128), F32)],
        cost_estimate=pl.CostEstimate(flops=2_000_000_000, bytes_accessed=1_000_000, transcendentals=0),
        compiler_params=PARAMS, name="term",
    )(blocks, known, adjacent, wanted, ranks)
    square, near = pl.pallas_call(
        square_kernel,
        out_shape=(like(ZH, TILES, BLK), like(2 * TILES, BLK)),
        in_specs=[SMEM] + [VMEM] * 3, out_specs=(VMEM, VMEM),
        scratch_shapes=[pltpu.VMEM((BLK, BLK), F32)], compiler_params=PARAMS, name="square",
    )(lists, own, left, right)
    square = swap(square, "zh").reshape(ZH * TILES, BLK)
    send = pl.pallas_call(
        send_kernel,
        out_shape=like(Y, ROOM * BLK, BLK),
        in_specs=[SMEM, VMEM], out_specs=VMEM, compiler_params=PARAMS, name="send",
    )(lists, square)
    result, level = pl.pallas_call(
        cube_kernel,
        out_shape=(like(*x.shape), like(1, dtype=jnp.int32)),
        in_specs=[SMEM, SMEM] + [VMEM] * 4, out_specs=(VMEM, SMEM),
        scratch_shapes=[pltpu.VMEM((BLK, BLK), F32)], compiler_params=PARAMS, name="cube",
    )(lists, blocks, own, left, near, swap(send, "y").reshape(Y * ROOM * BLK, BLK))
    result, level, x, blocks = lax.optimization_barrier((result, level, x, blocks))
    return lax.cond(level[0] > 0, lambda: general(x, blocks), lambda: result)


def solution(mesh):
    fine = Mesh(mesh.devices.reshape(ZH, Y, ZL, X, C), ROW + COL)
    return jax.shard_map(
        per_device,
        mesh=fine,
        in_specs=(P(ROW, COL), P(ROW, COL)),
        out_specs=P(ROW, COL),
        check_vma=False,
    )
```

```python
import jax
import jax.numpy as jnp
from jax import lax
from jax.experimental import pallas as pl
from jax.experimental.pallas import tpu as pltpu
from jax.sharding import Mesh, PartitionSpec as P

BLK = 128
NB = 384
ZH, Y, ZL, X, C = 3, 8, 4, 4, 2
XC = X * C
N_ROW, N_COL = ZH * Y, ZL * XC
SLOTS = 3
TILES = SLOTS * BLK
HEAD = 16
PANEL = TILES + HEAD
SLOTS_ROW = XC * SLOTS
LEFTS = ZL * SLOTS + SLOTS
OWN, PLAIN = 128, 160
ROOM = 2
ZROOM = 2
ZLIST, TERMS = 8, 16
ROW = ("zh", "y")
COL = ("zl", "x", "c")
F32 = jnp.float32
BF16 = jnp.bfloat16
PARAMS = pltpu.CompilerParams(vmem_limit_bytes=48 * 1024 * 1024)
VMEM = pl.BlockSpec(memory_space=pltpu.VMEM)
SMEM = pl.BlockSpec(memory_space=pltpu.SMEM)


def partner(fold_rows, fold_cols, keep_rows, keep_cols, out_rows, out_cols):
    folded_r = fold_rows[:, None, None]
    folded_c = fold_cols[:, None, None]
    kept_r = keep_rows[None, None, :]
    kept_c = keep_cols[None, None, :]
    target_r = out_rows[None, :, None]
    target_c = out_cols[None, :, None]
    linked = (folded_r == target_r) & (folded_c == kept_r) & (kept_c == target_c)
    linked = linked & (folded_r >= 0) & (kept_r >= 0) & (target_r >= 0)
    positions = jnp.arange(keep_rows.shape[0], dtype=jnp.int32)[None, None, :]
    partner_slot = jnp.sum(jnp.where(linked, positions, 0), axis=2)
    return (partner_slot, jnp.any(linked, axis=2))


def columns(tile_array, tile_blocks):
    return (
        lax.all_gather(tile_array, ROW, axis=0, tiled=True),
        lax.all_gather(tile_blocks, ROW, axis=0, tiled=True),
    )


def left_fold(left_tiles, tile_blocks, panel, panel_blocks):
    block_size = left_tiles.shape[0]
    slot_count = tile_blocks.shape[1]
    panel_rows = panel.shape[0] // block_size
    right_grid = panel.reshape(panel_rows, block_size, slot_count, block_size)
    kept_blocks = panel_blocks.reshape(panel_rows, 2, slot_count)
    kept_rows = kept_blocks[:, 0].reshape(-1)
    kept_cols = kept_blocks[:, 1].reshape(-1)
    piece_tiles = lax.all_gather(left_tiles, COL, axis=1, tiled=True)
    piece_blocks = lax.all_gather(tile_blocks, COL, axis=1, tiled=True)
    piece_slots = piece_blocks.shape[1]
    left_list = piece_tiles.reshape(block_size, piece_slots, block_size)
    partner_slot, matched = partner(
        piece_blocks[0], piece_blocks[1], kept_rows, kept_cols, tile_blocks[0], tile_blocks[1]
    )
    picked = right_grid[partner_slot // slot_count, :, partner_slot % slot_count, :]
    picked = picked * matched[:, :, None, None].astype(BF16)
    running = jnp.einsum("iak,aokj->ioj", left_list, picked, preferred_element_type=F32)
    return running.reshape(block_size, slot_count * block_size)


def general(iterate_tiles, tile_blocks):
    block_size = iterate_tiles.shape[0]
    slot_count = tile_blocks.shape[1]
    panel, panel_blocks = columns(iterate_tiles, tile_blocks)
    square = left_fold(iterate_tiles, tile_blocks, panel, panel_blocks).astype(BF16)
    panel, panel_blocks = columns(square, tile_blocks)
    cube = left_fold(iterate_tiles, tile_blocks, panel, panel_blocks)
    used = tile_blocks[0] >= 0
    updated = 1.5 * iterate_tiles.astype(F32) - 0.5 * cube
    shaped = updated.reshape(block_size, slot_count, block_size)
    kept = jnp.where(used[None, :, None], shaped, jnp.zeros_like(shaped))
    return kept.reshape(block_size, slot_count * block_size).astype(BF16)


def place():
    zh, y, zl = lax.axis_index("zh"), lax.axis_index("y"), lax.axis_index("zl")
    u = lax.axis_index("x") * C + lax.axis_index("c")
    return zh, y, zl, u, zh * Y + y, zl * XC + u


def iota(shape, dim):
    return lax.broadcasted_iota(jnp.int32, shape, dim)


def dot(a, b):
    return jnp.dot(a, b, preferred_element_type=F32)


def onehot(mask):
    return jnp.where(mask, 1.0, 0.0).astype(BF16)


def row_of(number):
    return number - N_ROW * ((number * 683) >> 14)


def col_of(number):
    return (number + ((number * 683) >> 14)) & (N_COL - 1)


def pack_kernel(blocks, x_ref, out_ref, own_ref):
    zh, y, zl, u, p, q = place()
    lane = iota((HEAD, 128), 1)
    here = iota((HEAD, 128), 0) == zh
    head = jnp.zeros((HEAD, 128), F32)
    for s in range(SLOTS):
        for v in range(4):
            number = blocks[v // 2, s]
            part = (number >> 4) if v % 2 == 0 else (number & 15)
            head = jnp.where(here & (lane == v * 32 + u * SLOTS + s), part.astype(F32), head)
    head = head.astype(BF16)
    for s in range(SLOTS):
        tile = x_ref[:, s * BLK : (s + 1) * BLK]
        own_ref[s * BLK : (s + 1) * BLK, :] = tile
        for z in range(ZH):
            out_ref[z, s * BLK : (s + 1) * BLK, :] = tile
    for z in range(ZH):
        out_ref[z, TILES:, :] = head


def row_tiles(gij_ref, p, lane):
    li = jnp.full((1, 128), -1.0, F32)
    lk = jnp.full((1, 128), -1.0, F32)
    for z in range(ZL):
        here = (lane >> 5 == z) & ((lane & 31) < SLOTS_ROW)
        mine = jnp.broadcast_to(gij_ref[pl.ds(z * 32 + p, 1), :], (8, 128))
        li = jnp.where(here, (pltpu.roll(mine, z * 32, 1) if z else mine)[0:1], li)
        lk = jnp.where(here, pltpu.roll(mine, (64 + z * 32) % 128, 1)[0:1], lk)
    return li, lk


def left_kernel(
    g_ref, second_ref, zbuf_ref, gij_ref, adj_ref, dl_ref, rl_ref,
    ohi_ref, ohj_ref, list_ref, list_smem, sem,
):
    zh, y, zl, u, p, q = place()
    told = g_ref[...].astype(F32)
    for z in range(ZL):
        for h in range(ZH):
            gij_ref[z * 32 + h * Y : z * 32 + (h + 1) * Y, :] = told[:, z * HEAD + h, :]
        gij_ref[z * 32 + N_ROW : (z + 1) * 32, :] = jnp.zeros((32 - N_ROW, 128), F32)
    g = gij_ref[...]
    g = 16.0 * g + pltpu.roll(g, 96, 1)
    row128, lane128 = iota((128, 128), 0), iota((128, 128), 1)
    g = jnp.where(((row128 & 31) < N_ROW) & ((lane128 & 63) < SLOTS_ROW), g, -1.0)
    gij_ref[...] = g
    gt = g.T
    sub = iota((NB, 128), 0).astype(F32)
    wide = iota((128, NB), 1).astype(F32)
    for k in range(SLOTS_ROW):
        ohi_ref[:, k * 128 : (k + 1) * 128] = onehot(sub == gt[k : k + 1, :])
        ohj_ref[k * 128 : (k + 1) * 128, :] = onehot(wide == g[:, 64 + k : 65 + k])
    adj_b = dot(ohi_ref[...], ohj_ref[...]).astype(BF16)
    adj_ref[...] = adj_b
    lane = iota((1, 128), 1)
    rows, lanes = iota((32, 128), 0), iota((32, 128), 1)
    rows8, lanes8 = iota((8, 128), 0), iota((8, 128), 1)
    in_col = onehot(col_of(iota((32, NB), 1)) == iota((32, NB), 0))

    li, lk = row_tiles(gij_ref, p, lane)
    stack = jnp.where(row128 == 0, li, lk).T
    both = dot(onehot(wide == stack[:, 0:1]), adj_b) * dot(onehot(wide == stack[:, 1:2]), adj_b)
    count = lax.dot_general(in_col, both.astype(BF16), (((1,), (1,)), ((), ())), preferred_element_type=F32)
    owner = (lanes >> 5) * XC + (((lanes & 31) * 11) >> 5)
    wanted = (count > 0.5) & (owner != rows) & ((lanes & 31) < SLOTS_ROW)
    wanted = jnp.where(wanted, 1.0, 0.0)
    dl_ref[...] = wanted
    rl_ref[...] = dot(wanted.astype(BF16), onehot((row128 < lane128) & ((row128 >> 5) == (lane128 >> 5))))
    send_d = jnp.zeros((8, 128), F32)
    send_r = jnp.zeros((8, 128), F32)
    for z in range(ZL):
        send_d = jnp.where(rows8 == z, dl_ref[pl.ds(z * XC + u, 1), :], send_d)
        send_r = jnp.where(rows8 == z, rl_ref[pl.ds(z * XC + u, 1), :], send_r)
    zlist = jnp.zeros((8, 128), F32)
    for c in range(SLOTS):
        hit = (send_d > 0.5) & (send_r == float(c)) & ((lanes8 >> 5) == zl)
        code = jnp.sum(jnp.where(hit, ((lanes8 & 31) + 1).astype(F32), 0.0), axis=1, keepdims=True)
        zlist = jnp.where(lanes8 == c, code, zlist)

    list_ref[...] = zlist.astype(jnp.int32)
    copy = pltpu.make_async_copy(list_ref, list_smem, sem)
    copy.start()
    copy.wait()
    for d in range(ZL):
        for c in range(SLOTS):
            code = list_smem[d, c]

            @pl.when(code > 0)
            def _():
                k = code - 1
                src_u = (k * 11) >> 5
                start = pl.multiple_of(src_u * PANEL + (k - src_u * SLOTS) * BLK, 16)
                zbuf_ref[d, c * BLK : (c + 1) * BLK, :] = second_ref[pl.ds(start, BLK), :]


def term_kernel(
    blocks, gij_ref, adj_ref, dl_ref, rl_ref, list_ref, gt_ref, dy_ref, ry_ref,
):
    zh, y, zl, u, p, q = place()
    gt_ref[...] = gij_ref[...].T
    row128, lane128 = iota((128, 128), 0), iota((128, 128), 1)
    sub = iota((NB, 128), 0).astype(F32)
    adj_b = adj_ref[...]
    adj = adj_b.astype(F32)
    adj_t = adj.T
    mutual = adj * adj_t
    lane = iota((1, 128), 1)
    lanes = iota((32, 128), 1)
    rows = iota((32, 128), 0)
    in_row = onehot(row_of(iota((32, NB), 1)) == iota((32, NB), 0))
    in_col_t = onehot(col_of(iota((NB, 32), 0)) == iota((NB, 32), 1))

    ci = jnp.full((1, 128), -1.0, F32)
    cj = jnp.full((1, 128), -1.0, F32)
    for s in range(SLOTS):
        shift = (s * 32 + 128 - zl * 32) & 127
        here = (lane >> 5 == s) & ((lane & 31) < N_ROW)
        rows_i = jnp.broadcast_to(gt_ref[pl.ds(u * SLOTS + s, 1), :], (8, 128))
        rows_j = jnp.broadcast_to(gt_ref[pl.ds(64 + u * SLOTS + s, 1), :], (8, 128))
        ci = jnp.where(here, pltpu.roll(rows_i, shift, 1)[0:1], ci)
        cj = jnp.where(here, pltpu.roll(rows_j, shift, 1)[0:1], cj)
    of_i = onehot(sub == ci)
    both = dot(adj_b, onehot(sub == cj)) * dot(adj_b, of_i)
    pairs = jnp.broadcast_to(jnp.sum(mutual, axis=0, keepdims=True), (8, NB)).astype(BF16)
    plain = (ci == cj) & (ci >= 0.0) & (dot(pairs, of_i)[0:1] < 1.5)
    plain_f = jnp.where(plain, 1.0, 0.0)
    wanted = (dot(in_row, both.astype(BF16)) > 0.5) & ((lanes & 31) != rows) & (plain_f < 0.5)
    wanted = jnp.where(wanted, 1.0, 0.0)
    dy_ref[...] = wanted
    ry_ref[...] = dot(wanted.astype(BF16), onehot((row128 < lane128) & ((row128 & 7) == (lane128 & 7))))
    lanes8 = iota((8, 128), 1)
    rows8 = iota((8, 128), 0)
    plane_d = jnp.zeros((8, 128), F32)
    for z in range(ZH):
        plane = jnp.max(wanted[z * Y : (z + 1) * Y], axis=0, keepdims=True)
        plane_d = jnp.where(rows8 == z, plane, plane_d)
    plane_r = dot(plane_d.astype(BF16), onehot((row128 < lane128) & ((row128 & 31) == (lane128 & 31))))
    place_z = jnp.sum(jnp.where(rows8 == zh, plane_r, 0.0), axis=0, keepdims=True)
    place_z = place_z + (((lane & 31) >> 3) * ZROOM + 1).astype(F32)
    send_d = dy_ref[pl.ds(pl.multiple_of(zh * Y, 8), 8), :]
    send_r = ry_ref[pl.ds(pl.multiple_of(zh * Y, 8), 8), :]
    ylist = jnp.zeros((8, 128), F32)
    for c in range(ROOM):
        hit = (send_d > 0.5) & (send_r == float(c)) & ((lanes8 & 7) == y)
        code = jnp.sum(jnp.where(hit, place_z, 0.0), axis=1, keepdims=True)
        ylist = jnp.where(lanes8 == c, code, ylist)
    for c in range(ZROOM):
        hit = (plane_d > 0.5) & (plane_r == float(c)) & ((lanes8 & 31) == p)
        code = jnp.sum(jnp.where(hit, ((lanes8 >> 5) + 1).astype(F32), 0.0), axis=1, keepdims=True)
        ylist = jnp.where(lanes8 == 8 + c, code, ylist)

    li, lk = row_tiles(gij_ref, p, lane)

    right = jnp.where(ci >= 0.0, (lane + 1).astype(F32), 0.0)
    got_d, got_r = dy_ref[pl.ds(p, 1), :], ry_ref[pl.ds(p, 1), :]
    again = jnp.where(got_d > 0.5, ((lane & 7) * ROOM + 1).astype(F32) + got_r, 0.0)
    again = jnp.where(plain, float(PLAIN), again)
    again = jnp.where(((lane & 31) == p) & (ci >= 0.0), (OWN + (lane >> 5)).astype(F32), again)
    stack = jnp.where(row128 == 0, ci, jnp.where(row128 == 1, cj, jnp.where(row128 == 2, right, again))).T
    ci_c, cj_c = stack[:, 0:1], stack[:, 1:2]
    met_c = ci_c == lk
    linked = (jnp.where(met_c, stack[:, 2:3], 0.0), jnp.where(met_c, stack[:, 3:4], 0.0))
    meets = [jnp.zeros((8, 128), F32), jnp.zeros((8, 128), F32)]
    terms = jnp.zeros((8, 128), F32)
    for o in range(SLOTS):
        out_i, out_j = blocks[0, o].astype(F32), blocks[1, o].astype(F32)
        for n in range(2):
            met = jnp.sum(jnp.where(cj_c == out_j, linked[n], 0.0), axis=0, keepdims=True)
            meets[n] = jnp.where(rows8 == o, jnp.where(li == out_i, met, 0.0), meets[n])
        hit = plain & (ci == out_j) & ((lane & 31) != p)
        code = jnp.sum(jnp.where(hit, (lane + 1).astype(F32), 0.0), axis=1, keepdims=True)
        terms = jnp.where((rows8 == o) & (lanes8 == 64), code, terms)
    got_d, got_r = dl_ref[pl.ds(q, 1), :], rl_ref[pl.ds(q, 1), :]
    for t in range(LEFTS):
        if t < ZL * SLOTS:
            hit = (lane >> 5 == t // SLOTS) & (got_d > 0.5) & (got_r == float(t % SLOTS))
        else:
            hit = lane == zl * 32 + u * SLOTS + (t - ZL * SLOTS)
        for n in range(2):
            value = jnp.sum(jnp.where(hit, meets[n], 0.0), axis=1, keepdims=True)
            terms = jnp.where(lanes8 == n * 32 + t, value, terms)

    def per_dev(count):
        return dot(dot(in_row, (count * adj).astype(BF16)).astype(BF16), in_col_t)

    from_i, from_k = iota((NB, NB), 0), iota((NB, NB), 1)
    k_row = row_of(iota((1, NB), 1))
    k_col = col_of(iota((1, NB), 1))
    i_row = row_of(iota((NB, 1), 0))
    i_col = col_of(iota((NB, 1), 0))
    def fullest(total, parts, room):
        least = total
        for part in parts:
            least = jnp.minimum(least, jnp.maximum(part, total - part))
        return jnp.max(jnp.where(least > room + 0.5, 1.0, 0.0), keepdims=True)

    to_col = jnp.where(i_col != k_col, adj, 0.0).astype(BF16)
    total = per_dev(dot(adj_b, to_col))
    parts = [
        per_dev(dot(jnp.where(((k_col >> bit) & 1) == 1, adj, 0.0).astype(BF16), to_col)) for bit in (3, 4)
    ]
    over = fullest(total, parts, SLOTS)
    moving = jnp.where(i_row != k_row, adj, 0.0)
    single = jnp.sum(mutual, axis=1, keepdims=True) < 1.5
    target = jnp.where((from_i == from_k) & single, 0.0, adj).astype(BF16)
    total = per_dev(dot(moving.astype(BF16), target))
    parts = [
        per_dev(dot(jnp.where(((k_row >> bit) & 1) == 1, moving, 0.0).astype(BF16), target)) for bit in (0, 1, 2)
    ]
    over = jnp.maximum(over, fullest(total, parts, ROOM))
    asked = dot(jnp.where(i_row != k_row, adj_t, 0.0).astype(BF16), adj_b) * target.astype(F32)
    asked = dot(dot(in_row, onehot(asked > 0.5)).astype(BF16), in_col_t)
    over = jnp.maximum(over, fullest(asked, [], ZROOM))
    level = jnp.where((rows8 == 7) & (lanes8 == 0), over, 0.0)

    list_ref[0:ZLIST, :] = ylist.astype(jnp.int32)
    list_ref[ZLIST:TERMS, :] = level.astype(jnp.int32)
    list_ref[TERMS:, :] = terms.astype(jnp.int32)


def tile_at(start):
    return pl.ds(pl.multiple_of(start, 16), BLK)


def left_at(t, left_ref, own_ref):
    if t < ZL * SLOTS:
        return left_ref.at[t * BLK : (t + 1) * BLK, :]
    t -= ZL * SLOTS
    return own_ref.at[t * BLK : (t + 1) * BLK, :]


def panel_start(code):
    r = code - 1
    return ((r & 7) * ZH + ((r >> 3) & 3)) * PANEL + (r >> 5) * BLK


def square_kernel(lists, own_ref, left_ref, right_ref, out_ref, near_ref, acc_ref):
    for o in range(SLOTS):
        part = slice(o * BLK, (o + 1) * BLK)
        acc_ref[...] = jnp.zeros((BLK, BLK), F32)
        for t in range(LEFTS):
            code = lists[TERMS + o, t]
            left = left_at(t, left_ref, own_ref)

            @pl.when(code > 0)
            def _():
                acc_ref[...] += dot(left[...], right_ref[tile_at(panel_start(code)), :])

        tile = acc_ref[...].astype(BF16)
        near_ref[part, :] = tile
        code = lists[TERMS + o, 64]

        @pl.when(code > 0)
        def _():
            tile = right_ref[tile_at(panel_start(code)), :]
            near_ref[TILES + o * BLK : TILES + (o + 1) * BLK, :] = dot(tile, tile).astype(BF16)

    for z in range(ZH):
        for c in range(ZROOM):
            code = lists[z, 8 + c]

            @pl.when((code > 0) & (code <= SLOTS))
            def _():
                out_ref[z, c * BLK : (c + 1) * BLK, :] = near_ref[tile_at((code - 1) * BLK), :]


def send_kernel(lists, square_ref, send_ref):
    for d in range(Y):
        for c in range(ROOM):
            code = lists[d, c]

            @pl.when((code > 0) & (code <= ZH * ZROOM))
            def _():
                send_ref[d, c * BLK : (c + 1) * BLK, :] = square_ref[tile_at((code - 1) * BLK), :]


def cube_kernel(lists, blocks, own_ref, left_ref, near_ref, right_ref, out_ref, level_ref, acc_ref):
    for o in range(SLOTS):
        part = slice(o * BLK, (o + 1) * BLK)
        acc_ref[...] = jnp.zeros((BLK, BLK), F32)
        for t in range(LEFTS):
            code = lists[TERMS + o, 32 + t]
            left = left_at(t, left_ref, own_ref)

            @pl.when((code > 0) & (code <= Y * ROOM))
            def _():
                acc_ref[...] += dot(left[...], right_ref[tile_at((code - 1) * BLK), :])

            @pl.when(code >= OWN)
            def _():
                start = jnp.where(code == PLAIN, TILES + o * BLK, (code - OWN) * BLK)
                acc_ref[...] += dot(left[...], near_ref[tile_at(start), :])

        value = 1.5 * own_ref[part, :].astype(F32) - 0.5 * acc_ref[...]
        out_ref[:, part] = jnp.where(blocks[0, o] >= 0, value, 0.0).astype(BF16)
    level_ref[0] = lists[TERMS - 1, 0]


def swap(value, axes):
    return lax.all_to_all(value, axes, 0, 0, tiled=True)


def like(*shape, dtype=BF16):
    return jax.ShapeDtypeStruct(shape, dtype)


def per_device(x, blocks):
    first, own = pl.pallas_call(
        pack_kernel,
        out_shape=(like(ZH, PANEL, BLK), like(TILES, BLK)),
        in_specs=[SMEM, VMEM], out_specs=(VMEM, VMEM), compiler_params=PARAMS, name="pack",
    )(blocks, x)
    first = swap(first, "zh")
    right = lax.all_gather(first.reshape(ZH * PANEL, BLK), "y", axis=0, tiled=True)
    heads = jnp.sum(first[:, TILES:].astype(F32), axis=0).astype(BF16)
    second = lax.all_gather(jnp.concatenate([own, heads], axis=0), ("x", "c"), axis=0)
    heads = jnp.sum(second[:, TILES:].astype(F32), axis=0).astype(BF16)
    heads = jnp.broadcast_to(heads[None], (Y * ZL, HEAD, 128)).reshape(Y * ZL * HEAD, 128)
    heads = swap(heads, ("y", "zl")).reshape(Y, ZL * HEAD, 128)
    zbuf, known, adjacent, wanted, ranks = pl.pallas_call(
        left_kernel,
        out_shape=(
            like(ZL, TILES, BLK), like(128, 128, dtype=F32), like(NB, NB),
            like(32, 128, dtype=F32), like(32, 128, dtype=F32),
        ),
        in_specs=[VMEM, VMEM], out_specs=(VMEM,) * 5,
        scratch_shapes=[
            pltpu.VMEM((NB, SLOTS_ROW * 128), BF16), pltpu.VMEM((SLOTS_ROW * 128, NB), BF16),
            pltpu.VMEM((8, 128), jnp.int32), pltpu.SMEM((8, 128), jnp.int32), pltpu.SemaphoreType.DMA,
        ],
        compiler_params=PARAMS, name="left",
    )(heads, second.reshape(XC * PANEL, BLK))
    left = swap(zbuf, "zl").reshape(ZL * TILES, BLK)
    lists = pl.pallas_call(
        term_kernel,
        out_shape=like(TERMS + 8, 128, dtype=jnp.int32),
        in_specs=[SMEM] + [VMEM] * 4, out_specs=VMEM,
        scratch_shapes=[pltpu.VMEM((128, 128), F32), pltpu.VMEM((32, 128), F32), pltpu.VMEM((32, 128), F32)],
        cost_estimate=pl.CostEstimate(flops=2_000_000_000, bytes_accessed=1_000_000, transcendentals=0),
        compiler_params=PARAMS, name="term",
    )(blocks, known, adjacent, wanted, ranks)
    square, near = pl.pallas_call(
        square_kernel,
        out_shape=(like(ZH, ZROOM * BLK, BLK), like(2 * TILES, BLK)),
        in_specs=[SMEM] + [VMEM] * 3, out_specs=(VMEM, VMEM),
        scratch_shapes=[pltpu.VMEM((BLK, BLK), F32)], compiler_params=PARAMS, name="square",
    )(lists, own, left, right)
    square = swap(square, "zh").reshape(ZH * ZROOM * BLK, BLK)
    send = pl.pallas_call(
        send_kernel,
        out_shape=like(Y, ROOM * BLK, BLK),
        in_specs=[SMEM, VMEM], out_specs=VMEM, compiler_params=PARAMS, name="send",
    )(lists, square)
    result, level = pl.pallas_call(
        cube_kernel,
        out_shape=(like(*x.shape), like(1, dtype=jnp.int32)),
        in_specs=[SMEM, SMEM] + [VMEM] * 4, out_specs=(VMEM, SMEM),
        scratch_shapes=[pltpu.VMEM((BLK, BLK), F32)], compiler_params=PARAMS, name="cube",
    )(lists, blocks, own, left, near, swap(send, "y").reshape(Y * ROOM * BLK, BLK))
    result, level, x, blocks = lax.optimization_barrier((result, level, x, blocks))
    return lax.cond(level[0] > 0, lambda: general(x, blocks), lambda: result)


def solution(mesh):
    fine = Mesh(mesh.devices.reshape(ZH, Y, ZL, X, C), ROW + COL)
    return jax.shard_map(
        per_device,
        mesh=fine,
        in_specs=(P(ROW, COL), P(ROW, COL)),
        out_specs=P(ROW, COL),
        check_vma=False,
    )
```

```python
import jax
import jax.numpy as jnp
from jax import lax
from jax.experimental import pallas as pl
from jax.experimental.pallas import tpu as pltpu
from jax.sharding import Mesh, PartitionSpec as P

BLK = 128
NB = 384
ZH, Y, ZL, X, C = 3, 8, 4, 4, 2
XC = X * C
N_ROW, N_COL = ZH * Y, ZL * XC
SLOTS = 3
TILES = SLOTS * BLK
HEAD = 16
PANEL = TILES + HEAD
SLOTS_ROW = XC * SLOTS
LEFTS = ZL * SLOTS + SLOTS
OWN, PLAIN = 128, 160
ROOM = 2
ZROOM = 2
ZLIST, TERMS = 8, 16
ROW = ("zh", "y")
COL = ("zl", "x", "c")
F32 = jnp.float32
BF16 = jnp.bfloat16
PARAMS = pltpu.CompilerParams(vmem_limit_bytes=48 * 1024 * 1024)
VMEM = pl.BlockSpec(memory_space=pltpu.VMEM)
SMEM = pl.BlockSpec(memory_space=pltpu.SMEM)


def partner(fold_rows, fold_cols, keep_rows, keep_cols, out_rows, out_cols):
    folded_r = fold_rows[:, None, None]
    folded_c = fold_cols[:, None, None]
    kept_r = keep_rows[None, None, :]
    kept_c = keep_cols[None, None, :]
    target_r = out_rows[None, :, None]
    target_c = out_cols[None, :, None]
    linked = (folded_r == target_r) & (folded_c == kept_r) & (kept_c == target_c)
    linked = linked & (folded_r >= 0) & (kept_r >= 0) & (target_r >= 0)
    positions = jnp.arange(keep_rows.shape[0], dtype=jnp.int32)[None, None, :]
    partner_slot = jnp.sum(jnp.where(linked, positions, 0), axis=2)
    return (partner_slot, jnp.any(linked, axis=2))


def columns(tile_array, tile_blocks):
    return (
        lax.all_gather(tile_array, ROW, axis=0, tiled=True),
        lax.all_gather(tile_blocks, ROW, axis=0, tiled=True),
    )


def left_fold(left_tiles, tile_blocks, panel, panel_blocks):
    block_size = left_tiles.shape[0]
    slot_count = tile_blocks.shape[1]
    panel_rows = panel.shape[0] // block_size
    right_grid = panel.reshape(panel_rows, block_size, slot_count, block_size)
    kept_blocks = panel_blocks.reshape(panel_rows, 2, slot_count)
    kept_rows = kept_blocks[:, 0].reshape(-1)
    kept_cols = kept_blocks[:, 1].reshape(-1)
    piece_tiles = lax.all_gather(left_tiles, COL, axis=1, tiled=True)
    piece_blocks = lax.all_gather(tile_blocks, COL, axis=1, tiled=True)
    piece_slots = piece_blocks.shape[1]
    left_list = piece_tiles.reshape(block_size, piece_slots, block_size)
    partner_slot, matched = partner(
        piece_blocks[0], piece_blocks[1], kept_rows, kept_cols, tile_blocks[0], tile_blocks[1]
    )
    picked = right_grid[partner_slot // slot_count, :, partner_slot % slot_count, :]
    picked = picked * matched[:, :, None, None].astype(BF16)
    running = jnp.einsum("iak,aokj->ioj", left_list, picked, preferred_element_type=F32)
    return running.reshape(block_size, slot_count * block_size)


def general(iterate_tiles, tile_blocks):
    block_size = iterate_tiles.shape[0]
    slot_count = tile_blocks.shape[1]
    panel, panel_blocks = columns(iterate_tiles, tile_blocks)
    square = left_fold(iterate_tiles, tile_blocks, panel, panel_blocks).astype(BF16)
    panel, panel_blocks = columns(square, tile_blocks)
    cube = left_fold(iterate_tiles, tile_blocks, panel, panel_blocks)
    used = tile_blocks[0] >= 0
    updated = 1.5 * iterate_tiles.astype(F32) - 0.5 * cube
    shaped = updated.reshape(block_size, slot_count, block_size)
    kept = jnp.where(used[None, :, None], shaped, jnp.zeros_like(shaped))
    return kept.reshape(block_size, slot_count * block_size).astype(BF16)


def place():
    zh, y, zl = lax.axis_index("zh"), lax.axis_index("y"), lax.axis_index("zl")
    u = lax.axis_index("x") * C + lax.axis_index("c")
    return zh, y, zl, u, zh * Y + y, zl * XC + u


def iota(shape, dim):
    return lax.broadcasted_iota(jnp.int32, shape, dim)


def dot(a, b):
    return jnp.dot(a, b, preferred_element_type=F32)


def onehot(mask):
    return jnp.where(mask, 1.0, 0.0).astype(BF16)


def row_of(number):
    return number - N_ROW * ((number * 683) >> 14)


def col_of(number):
    return (number + ((number * 683) >> 14)) & (N_COL - 1)


def pack_kernel(blocks, x_ref, out_ref, own_ref):
    zh, y, zl, u, p, q = place()
    lane = iota((HEAD, 128), 1)
    here = iota((HEAD, 128), 0) == zh
    head = jnp.zeros((HEAD, 128), F32)
    for s in range(SLOTS):
        for v in range(4):
            number = blocks[v // 2, s]
            part = (number >> 4) if v % 2 == 0 else (number & 15)
            head = jnp.where(here & (lane == v * 32 + u * SLOTS + s), part.astype(F32), head)
    head = head.astype(BF16)
    for s in range(SLOTS):
        tile = x_ref[:, s * BLK : (s + 1) * BLK]
        own_ref[s * BLK : (s + 1) * BLK, :] = tile
        for z in range(ZH):
            out_ref[z, s * BLK : (s + 1) * BLK, :] = tile
    for z in range(ZH):
        out_ref[z, TILES:, :] = head


def row_tiles(gij_ref, p, lane):
    li = jnp.full((1, 128), -1.0, F32)
    lk = jnp.full((1, 128), -1.0, F32)
    for z in range(ZL):
        here = (lane >> 5 == z) & ((lane & 31) < SLOTS_ROW)
        mine = jnp.broadcast_to(gij_ref[pl.ds(z * 32 + p, 1), :], (8, 128))
        li = jnp.where(here, (pltpu.roll(mine, z * 32, 1) if z else mine)[0:1], li)
        lk = jnp.where(here, pltpu.roll(mine, (64 + z * 32) % 128, 1)[0:1], lk)
    return li, lk


def left_kernel(
    g_ref, second_ref, zbuf_ref, gij_ref, adj_ref, dl_ref, rl_ref,
    ohi_ref, ohj_ref, list_ref, list_smem, sem,
):
    zh, y, zl, u, p, q = place()
    told = g_ref[...].astype(F32)
    for z in range(ZL):
        for h in range(ZH):
            gij_ref[z * 32 + h * Y : z * 32 + (h + 1) * Y, :] = told[:, z * HEAD + h, :]
        gij_ref[z * 32 + N_ROW : (z + 1) * 32, :] = jnp.zeros((32 - N_ROW, 128), F32)
    g = gij_ref[...]
    g = 16.0 * g + pltpu.roll(g, 96, 1)
    row128, lane128 = iota((128, 128), 0), iota((128, 128), 1)
    g = jnp.where(((row128 & 31) < N_ROW) & ((lane128 & 63) < SLOTS_ROW), g, -1.0)
    gij_ref[...] = g
    gt = g.T
    sub = iota((NB, 128), 0).astype(F32)
    wide = iota((128, NB), 1).astype(F32)
    for k in range(SLOTS_ROW):
        ohi_ref[:, k * 128 : (k + 1) * 128] = onehot(sub == gt[k : k + 1, :])
        ohj_ref[k * 128 : (k + 1) * 128, :] = onehot(wide == g[:, 64 + k : 65 + k])
    adj_b = dot(ohi_ref[...], ohj_ref[...]).astype(BF16)
    adj_ref[...] = adj_b
    lane = iota((1, 128), 1)
    rows, lanes = iota((32, 128), 0), iota((32, 128), 1)
    rows8, lanes8 = iota((8, 128), 0), iota((8, 128), 1)
    in_col = onehot(col_of(iota((32, NB), 1)) == iota((32, NB), 0))

    li, lk = row_tiles(gij_ref, p, lane)
    stack = jnp.where(row128 == 0, li, lk).T
    both = dot(onehot(wide == stack[:, 0:1]), adj_b) * dot(onehot(wide == stack[:, 1:2]), adj_b)
    count = lax.dot_general(in_col, both.astype(BF16), (((1,), (1,)), ((), ())), preferred_element_type=F32)
    owner = (lanes >> 5) * XC + (((lanes & 31) * 11) >> 5)
    wanted = (count > 0.5) & (owner != rows) & ((lanes & 31) < SLOTS_ROW)
    wanted = jnp.where(wanted, 1.0, 0.0)
    dl_ref[...] = wanted
    rl_ref[...] = dot(wanted.astype(BF16), onehot((row128 < lane128) & ((row128 >> 5) == (lane128 >> 5))))
    send_d = jnp.zeros((8, 128), F32)
    send_r = jnp.zeros((8, 128), F32)
    for z in range(ZL):
        send_d = jnp.where(rows8 == z, dl_ref[pl.ds(z * XC + u, 1), :], send_d)
        send_r = jnp.where(rows8 == z, rl_ref[pl.ds(z * XC + u, 1), :], send_r)
    zlist = jnp.zeros((8, 128), F32)
    for c in range(SLOTS):
        hit = (send_d > 0.5) & (send_r == float(c)) & ((lanes8 >> 5) == zl)
        code = jnp.sum(jnp.where(hit, ((lanes8 & 31) + 1).astype(F32), 0.0), axis=1, keepdims=True)
        zlist = jnp.where(lanes8 == c, code, zlist)

    list_ref[...] = zlist.astype(jnp.int32)
    copy = pltpu.make_async_copy(list_ref, list_smem, sem)
    copy.start()
    copy.wait()
    for d in range(ZL):
        for c in range(SLOTS):
            code = list_smem[d, c]

            @pl.when(code > 0)
            def _():
                k = code - 1
                src_u = (k * 11) >> 5
                start = pl.multiple_of(src_u * PANEL + (k - src_u * SLOTS) * BLK, 16)
                zbuf_ref[d, c * BLK : (c + 1) * BLK, :] = second_ref[pl.ds(start, BLK), :]


def term_kernel(
    blocks, gij_ref, adj_ref, dl_ref, rl_ref, list_ref, gt_ref, dy_ref, ry_ref,
):
    zh, y, zl, u, p, q = place()
    gt_ref[...] = gij_ref[...].T
    row128, lane128 = iota((128, 128), 0), iota((128, 128), 1)
    sub = iota((NB, 128), 0).astype(F32)
    adj_b = adj_ref[...]
    adj = adj_b.astype(F32)
    adj_t = adj.T
    mutual = adj * adj_t
    lane = iota((1, 128), 1)
    lanes = iota((32, 128), 1)
    rows = iota((32, 128), 0)
    in_row = onehot(row_of(iota((32, NB), 1)) == iota((32, NB), 0))
    in_col_t = onehot(col_of(iota((NB, 32), 0)) == iota((NB, 32), 1))

    ci = jnp.full((1, 128), -1.0, F32)
    cj = jnp.full((1, 128), -1.0, F32)
    for s in range(SLOTS):
        shift = (s * 32 + 128 - zl * 32) & 127
        here = (lane >> 5 == s) & ((lane & 31) < N_ROW)
        rows_i = jnp.broadcast_to(gt_ref[pl.ds(u * SLOTS + s, 1), :], (8, 128))
        rows_j = jnp.broadcast_to(gt_ref[pl.ds(64 + u * SLOTS + s, 1), :], (8, 128))
        ci = jnp.where(here, pltpu.roll(rows_i, shift, 1)[0:1], ci)
        cj = jnp.where(here, pltpu.roll(rows_j, shift, 1)[0:1], cj)
    of_i = onehot(sub == ci)
    both = dot(adj_b, onehot(sub == cj)) * dot(adj_b, of_i)
    pairs = jnp.broadcast_to(jnp.sum(mutual, axis=0, keepdims=True), (8, NB)).astype(BF16)
    plain = (ci == cj) & (ci >= 0.0) & (dot(pairs, of_i)[0:1] < 1.5)
    plain_f = jnp.where(plain, 1.0, 0.0)
    wanted = (dot(in_row, both.astype(BF16)) > 0.5) & ((lanes & 31) != rows) & (plain_f < 0.5)
    wanted = jnp.where(wanted, 1.0, 0.0)
    dy_ref[...] = wanted
    ry_ref[...] = dot(wanted.astype(BF16), onehot((row128 < lane128) & ((row128 & 7) == (lane128 & 7))))
    lanes8 = iota((8, 128), 1)
    rows8 = iota((8, 128), 0)
    plane_d = jnp.zeros((8, 128), F32)
    for z in range(ZH):
        plane = jnp.max(wanted[z * Y : (z + 1) * Y], axis=0, keepdims=True)
        plane_d = jnp.where(rows8 == z, plane, plane_d)
    plane_r = dot(plane_d.astype(BF16), onehot((row128 < lane128) & ((row128 & 31) == (lane128 & 31))))
    place_z = jnp.sum(jnp.where(rows8 == zh, plane_r, 0.0), axis=0, keepdims=True)
    place_z = place_z + (((lane & 31) >> 3) * ZROOM + 1).astype(F32)
    send_d = dy_ref[pl.ds(pl.multiple_of(zh * Y, 8), 8), :]
    send_r = ry_ref[pl.ds(pl.multiple_of(zh * Y, 8), 8), :]
    ylist = jnp.zeros((8, 128), F32)
    for c in range(ROOM):
        hit = (send_d > 0.5) & (send_r == float(c)) & ((lanes8 & 7) == y)
        code = jnp.sum(jnp.where(hit, place_z, 0.0), axis=1, keepdims=True)
        ylist = jnp.where(lanes8 == c, code, ylist)
    for c in range(ZROOM):
        hit = (plane_d > 0.5) & (plane_r == float(c)) & ((lanes8 & 31) == p)
        code = jnp.sum(jnp.where(hit, ((lanes8 >> 5) + 1).astype(F32), 0.0), axis=1, keepdims=True)
        ylist = jnp.where(lanes8 == 8 + c, code, ylist)

    li, lk = row_tiles(gij_ref, p, lane)

    right = jnp.where(ci >= 0.0, (lane + 1).astype(F32), 0.0)
    got_d, got_r = dy_ref[pl.ds(p, 1), :], ry_ref[pl.ds(p, 1), :]
    again = jnp.where(got_d > 0.5, ((lane & 7) * ROOM + 1).astype(F32) + got_r, 0.0)
    again = jnp.where(plain, float(PLAIN), again)
    again = jnp.where(((lane & 31) == p) & (ci >= 0.0), (OWN + (lane >> 5)).astype(F32), again)
    stack = jnp.where(row128 == 0, ci, jnp.where(row128 == 1, cj, jnp.where(row128 == 2, right, again))).T
    ci_c, cj_c = stack[:, 0:1], stack[:, 1:2]
    met_c = ci_c == lk
    linked = (jnp.where(met_c, stack[:, 2:3], 0.0), jnp.where(met_c, stack[:, 3:4], 0.0))
    meets = [jnp.zeros((8, 128), F32), jnp.zeros((8, 128), F32)]
    terms = jnp.zeros((8, 128), F32)
    for o in range(SLOTS):
        out_i, out_j = blocks[0, o].astype(F32), blocks[1, o].astype(F32)
        for n in range(2):
            met = jnp.sum(jnp.where(cj_c == out_j, linked[n], 0.0), axis=0, keepdims=True)
            meets[n] = jnp.where(rows8 == o, jnp.where(li == out_i, met, 0.0), meets[n])
        hit = plain & (ci == out_j) & ((lane & 31) != p)
        code = jnp.sum(jnp.where(hit, (lane + 1).astype(F32), 0.0), axis=1, keepdims=True)
        terms = jnp.where((rows8 == o) & (lanes8 == 64), code, terms)
    got_d, got_r = dl_ref[pl.ds(q, 1), :], rl_ref[pl.ds(q, 1), :]
    for t in range(LEFTS):
        if t < ZL * SLOTS:
            hit = (lane >> 5 == t // SLOTS) & (got_d > 0.5) & (got_r == float(t % SLOTS))
        else:
            hit = lane == zl * 32 + u * SLOTS + (t - ZL * SLOTS)
        for n in range(2):
            value = jnp.sum(jnp.where(hit, meets[n], 0.0), axis=1, keepdims=True)
            terms = jnp.where(lanes8 == n * 32 + t, value, terms)

    def per_dev(count):
        return dot(dot(in_row, (count * adj).astype(BF16)).astype(BF16), in_col_t)

    from_i, from_k = iota((NB, NB), 0), iota((NB, NB), 1)
    k_row = row_of(iota((1, NB), 1))
    k_col = col_of(iota((1, NB), 1))
    i_row = row_of(iota((NB, 1), 0))
    i_col = col_of(iota((NB, 1), 0))
    def fullest(total, parts, room):
        least = total
        for part in parts:
            least = jnp.minimum(least, jnp.maximum(part, total - part))
        return jnp.max(jnp.where(least > room + 0.5, 1.0, 0.0), keepdims=True)

    to_col = jnp.where(i_col != k_col, adj, 0.0).astype(BF16)
    total = per_dev(dot(adj_b, to_col))
    parts = [
        per_dev(dot(jnp.where(((k_col >> bit) & 1) == 1, adj, 0.0).astype(BF16), to_col)) for bit in (3, 4)
    ]
    over = fullest(total, parts, SLOTS)
    moving = jnp.where(i_row != k_row, adj, 0.0)
    single = jnp.sum(mutual, axis=1, keepdims=True) < 1.5
    target = jnp.where((from_i == from_k) & single, 0.0, adj).astype(BF16)
    total = per_dev(dot(moving.astype(BF16), target))
    parts = [
        per_dev(dot(jnp.where(((k_row >> bit) & 1) == 1, moving, 0.0).astype(BF16), target)) for bit in (0, 1, 2)
    ]
    over = jnp.maximum(over, fullest(total, parts, ROOM))
    asked = dot(jnp.where(i_row != k_row, adj_t, 0.0).astype(BF16), adj_b) * target.astype(F32)
    asked = dot(dot(in_row, onehot(asked > 0.5)).astype(BF16), in_col_t)
    over = jnp.maximum(over, fullest(asked, [], ZROOM))
    level = jnp.where((rows8 == 7) & (lanes8 == 0), over, 0.0)

    list_ref[0:ZLIST, :] = ylist.astype(jnp.int32)
    list_ref[ZLIST:TERMS, :] = level.astype(jnp.int32)
    list_ref[TERMS:, :] = terms.astype(jnp.int32)


def tile_at(start):
    return pl.ds(pl.multiple_of(start, 16), BLK)


def left_at(t, left_ref, own_ref):
    if t < ZL * SLOTS:
        return left_ref.at[t * BLK : (t + 1) * BLK, :]
    t -= ZL * SLOTS
    return own_ref.at[t * BLK : (t + 1) * BLK, :]


def panel_start(code):
    r = code - 1
    return ((r & 7) * ZH + ((r >> 3) & 3)) * PANEL + (r >> 5) * BLK


def near_kernel(lists, own_ref, left_ref, near_ref, right_ref, sum_ref, diag_ref):
    for o in range(SLOTS):
        part = slice(o * BLK, (o + 1) * BLK)
        sum_ref[part, :] = jnp.zeros((BLK, BLK), F32)
        code = lists[TERMS + o, 64]

        @pl.when(code > 0)
        def _():
            tile = right_ref[tile_at(panel_start(code)), :]
            diag_ref[...] = dot(tile, tile).astype(BF16)

        for t in range(LEFTS):
            code = lists[TERMS + o, 32 + t]
            left = left_at(t, left_ref, own_ref)

            @pl.when((code >= OWN) & (code < PLAIN))
            def _():
                sum_ref[part, :] += dot(left[...], near_ref[tile_at((code - OWN) * BLK), :])

            @pl.when(code == PLAIN)
            def _():
                sum_ref[part, :] += dot(left[...], diag_ref[...])


def square_kernel(lists, own_ref, left_ref, right_ref, out_ref, near_ref, acc_ref):
    for o in range(SLOTS):
        part = slice(o * BLK, (o + 1) * BLK)
        acc_ref[...] = jnp.zeros((BLK, BLK), F32)
        for t in range(LEFTS):
            code = lists[TERMS + o, t]
            left = left_at(t, left_ref, own_ref)

            @pl.when(code > 0)
            def _():
                acc_ref[...] += dot(left[...], right_ref[tile_at(panel_start(code)), :])

        tile = acc_ref[...].astype(BF16)
        near_ref[part, :] = tile

    for z in range(ZH):
        for c in range(ZROOM):
            code = lists[z, 8 + c]

            @pl.when((code > 0) & (code <= SLOTS))
            def _():
                out_ref[z, c * BLK : (c + 1) * BLK, :] = near_ref[tile_at((code - 1) * BLK), :]


def send_kernel(lists, square_ref, send_ref):
    for d in range(Y):
        for c in range(ROOM):
            code = lists[d, c]

            @pl.when((code > 0) & (code <= ZH * ZROOM))
            def _():
                send_ref[d, c * BLK : (c + 1) * BLK, :] = square_ref[tile_at((code - 1) * BLK), :]


def cube_kernel(lists, blocks, own_ref, left_ref, sum_ref, right_ref, out_ref, level_ref, acc_ref):
    for o in range(SLOTS):
        part = slice(o * BLK, (o + 1) * BLK)
        acc_ref[...] = sum_ref[part, :]
        for t in range(LEFTS):
            code = lists[TERMS + o, 32 + t]
            left = left_at(t, left_ref, own_ref)

            @pl.when((code > 0) & (code <= Y * ROOM))
            def _():
                acc_ref[...] += dot(left[...], right_ref[tile_at((code - 1) * BLK), :])

        value = 1.5 * own_ref[part, :].astype(F32) - 0.5 * acc_ref[...]
        out_ref[:, part] = jnp.where(blocks[0, o] >= 0, value, 0.0).astype(BF16)
    level_ref[0] = lists[TERMS - 1, 0]


def swap(value, axes):
    return lax.all_to_all(value, axes, 0, 0, tiled=True)


def like(*shape, dtype=BF16):
    return jax.ShapeDtypeStruct(shape, dtype)


def per_device(x, blocks):
    first, own = pl.pallas_call(
        pack_kernel,
        out_shape=(like(ZH, PANEL, BLK), like(TILES, BLK)),
        in_specs=[SMEM, VMEM], out_specs=(VMEM, VMEM), compiler_params=PARAMS, name="pack",
    )(blocks, x)
    first = swap(first, "zh")
    right = lax.all_gather(first.reshape(ZH * PANEL, BLK), "y", axis=0, tiled=True)
    heads = jnp.sum(first[:, TILES:].astype(F32), axis=0).astype(BF16)
    second = lax.all_gather(jnp.concatenate([own, heads], axis=0), ("x", "c"), axis=0)
    heads = jnp.sum(second[:, TILES:].astype(F32), axis=0).astype(BF16)
    heads = jnp.broadcast_to(heads[None], (Y * ZL, HEAD, 128)).reshape(Y * ZL * HEAD, 128)
    heads = swap(heads, ("y", "zl")).reshape(Y, ZL * HEAD, 128)
    zbuf, known, adjacent, wanted, ranks = pl.pallas_call(
        left_kernel,
        out_shape=(
            like(ZL, TILES, BLK), like(128, 128, dtype=F32), like(NB, NB),
            like(32, 128, dtype=F32), like(32, 128, dtype=F32),
        ),
        in_specs=[VMEM, VMEM], out_specs=(VMEM,) * 5,
        scratch_shapes=[
            pltpu.VMEM((NB, SLOTS_ROW * 128), BF16), pltpu.VMEM((SLOTS_ROW * 128, NB), BF16),
            pltpu.VMEM((8, 128), jnp.int32), pltpu.SMEM((8, 128), jnp.int32), pltpu.SemaphoreType.DMA,
        ],
        compiler_params=PARAMS, name="left",
    )(heads, second.reshape(XC * PANEL, BLK))
    left = swap(zbuf, "zl").reshape(ZL * TILES, BLK)
    lists = pl.pallas_call(
        term_kernel,
        out_shape=like(TERMS + 8, 128, dtype=jnp.int32),
        in_specs=[SMEM] + [VMEM] * 4, out_specs=VMEM,
        scratch_shapes=[pltpu.VMEM((128, 128), F32), pltpu.VMEM((32, 128), F32), pltpu.VMEM((32, 128), F32)],
        cost_estimate=pl.CostEstimate(flops=2_000_000_000, bytes_accessed=1_000_000, transcendentals=0),
        compiler_params=PARAMS, name="term",
    )(blocks, known, adjacent, wanted, ranks)
    square, near = pl.pallas_call(
        square_kernel,
        out_shape=(like(ZH, ZROOM * BLK, BLK), like(TILES, BLK)),
        in_specs=[SMEM] + [VMEM] * 3, out_specs=(VMEM, VMEM),
        scratch_shapes=[pltpu.VMEM((BLK, BLK), F32)], compiler_params=PARAMS, name="square",
    )(lists, own, left, right)
    square = swap(square, "zh").reshape(ZH * ZROOM * BLK, BLK)
    send = pl.pallas_call(
        send_kernel,
        out_shape=like(Y, ROOM * BLK, BLK),
        in_specs=[SMEM, VMEM], out_specs=VMEM, compiler_params=PARAMS, name="send",
    )(lists, square)
    sums = pl.pallas_call(
        near_kernel,
        out_shape=like(TILES, BLK, dtype=F32),
        in_specs=[SMEM] + [VMEM] * 4, out_specs=VMEM,
        scratch_shapes=[pltpu.VMEM((BLK, BLK), BF16)],
        cost_estimate=pl.CostEstimate(flops=2_000_000_000, bytes_accessed=1_000_000, transcendentals=0),
        compiler_params=PARAMS, name="near",
    )(lists, own, left, near, right)
    result, level = pl.pallas_call(
        cube_kernel,
        out_shape=(like(*x.shape), like(1, dtype=jnp.int32)),
        in_specs=[SMEM, SMEM] + [VMEM] * 4, out_specs=(VMEM, SMEM),
        scratch_shapes=[pltpu.VMEM((BLK, BLK), F32)], compiler_params=PARAMS, name="cube",
    )(lists, blocks, own, left, sums, swap(send, "y").reshape(Y * ROOM * BLK, BLK))
    result, level, x, blocks = lax.optimization_barrier((result, level, x, blocks))
    return lax.cond(level[0] > 0, lambda: general(x, blocks), lambda: result)


def solution(mesh):
    fine = Mesh(mesh.devices.reshape(ZH, Y, ZL, X, C), ROW + COL)
    return jax.shard_map(
        per_device,
        mesh=fine,
        in_specs=(P(ROW, COL), P(ROW, COL)),
        out_specs=P(ROW, COL),
        check_vma=False,
    )
```

```python
import jax
import jax.numpy as jnp
from jax import lax
from jax.experimental import pallas as pl
from jax.experimental.pallas import tpu as pltpu
from jax.sharding import Mesh, PartitionSpec as P

BLK = 128
NB = 384
ZH, Y, ZL, X, C = 3, 8, 4, 4, 2
XC = X * C
N_ROW, N_COL = ZH * Y, ZL * XC
SLOTS = 3
TILES = SLOTS * BLK
HEAD = 16
PANEL = TILES + HEAD
SECOND = TILES + ZH * HEAD
SLOTS_ROW = XC * SLOTS
LEFTS = ZL * SLOTS + SLOTS
OWN, PLAIN = 128, 160
ROOM = 2
ZROOM = 2
ZLIST, TERMS = 8, 16
ROW = ("zh", "y")
COL = ("zl", "x", "c")
F32 = jnp.float32
BF16 = jnp.bfloat16
PARAMS = pltpu.CompilerParams(vmem_limit_bytes=48 * 1024 * 1024)
VMEM = pl.BlockSpec(memory_space=pltpu.VMEM)
SMEM = pl.BlockSpec(memory_space=pltpu.SMEM)


def partner(fold_rows, fold_cols, keep_rows, keep_cols, out_rows, out_cols):
    folded_r = fold_rows[:, None, None]
    folded_c = fold_cols[:, None, None]
    kept_r = keep_rows[None, None, :]
    kept_c = keep_cols[None, None, :]
    target_r = out_rows[None, :, None]
    target_c = out_cols[None, :, None]
    linked = (folded_r == target_r) & (folded_c == kept_r) & (kept_c == target_c)
    linked = linked & (folded_r >= 0) & (kept_r >= 0) & (target_r >= 0)
    positions = jnp.arange(keep_rows.shape[0], dtype=jnp.int32)[None, None, :]
    partner_slot = jnp.sum(jnp.where(linked, positions, 0), axis=2)
    return (partner_slot, jnp.any(linked, axis=2))


def columns(tile_array, tile_blocks):
    return (
        lax.all_gather(tile_array, ROW, axis=0, tiled=True),
        lax.all_gather(tile_blocks, ROW, axis=0, tiled=True),
    )


def left_fold(left_tiles, tile_blocks, panel, panel_blocks):
    block_size = left_tiles.shape[0]
    slot_count = tile_blocks.shape[1]
    panel_rows = panel.shape[0] // block_size
    right_grid = panel.reshape(panel_rows, block_size, slot_count, block_size)
    kept_blocks = panel_blocks.reshape(panel_rows, 2, slot_count)
    kept_rows = kept_blocks[:, 0].reshape(-1)
    kept_cols = kept_blocks[:, 1].reshape(-1)
    piece_tiles = lax.all_gather(left_tiles, COL, axis=1, tiled=True)
    piece_blocks = lax.all_gather(tile_blocks, COL, axis=1, tiled=True)
    piece_slots = piece_blocks.shape[1]
    left_list = piece_tiles.reshape(block_size, piece_slots, block_size)
    partner_slot, matched = partner(
        piece_blocks[0], piece_blocks[1], kept_rows, kept_cols, tile_blocks[0], tile_blocks[1]
    )
    picked = right_grid[partner_slot // slot_count, :, partner_slot % slot_count, :]
    picked = picked * matched[:, :, None, None].astype(BF16)
    running = jnp.einsum("iak,aokj->ioj", left_list, picked, preferred_element_type=F32)
    return running.reshape(block_size, slot_count * block_size)


def general(iterate_tiles, tile_blocks):
    block_size = iterate_tiles.shape[0]
    slot_count = tile_blocks.shape[1]
    panel, panel_blocks = columns(iterate_tiles, tile_blocks)
    square = left_fold(iterate_tiles, tile_blocks, panel, panel_blocks).astype(BF16)
    panel, panel_blocks = columns(square, tile_blocks)
    cube = left_fold(iterate_tiles, tile_blocks, panel, panel_blocks)
    used = tile_blocks[0] >= 0
    updated = 1.5 * iterate_tiles.astype(F32) - 0.5 * cube
    shaped = updated.reshape(block_size, slot_count, block_size)
    kept = jnp.where(used[None, :, None], shaped, jnp.zeros_like(shaped))
    return kept.reshape(block_size, slot_count * block_size).astype(BF16)


def place():
    zh, y, zl = lax.axis_index("zh"), lax.axis_index("y"), lax.axis_index("zl")
    u = lax.axis_index("x") * C + lax.axis_index("c")
    return zh, y, zl, u, zh * Y + y, zl * XC + u


def iota(shape, dim):
    return lax.broadcasted_iota(jnp.int32, shape, dim)


def dot(a, b):
    return jnp.dot(a, b, preferred_element_type=F32)


def onehot(mask):
    return jnp.where(mask, 1.0, 0.0).astype(BF16)


def row_of(number):
    return number - N_ROW * ((number * 683) >> 14)


def col_of(number):
    return (number + ((number * 683) >> 14)) & (N_COL - 1)


def pack_kernel(blocks, x_ref, out_ref, own_ref):
    zh, y, zl, u, p, q = place()
    lane = iota((HEAD, 128), 1)
    here = iota((HEAD, 128), 0) == zh
    head = jnp.zeros((HEAD, 128), F32)
    for s in range(SLOTS):
        for v in range(4):
            number = blocks[v // 2, s]
            part = (number >> 4) if v % 2 == 0 else (number & 15)
            head = jnp.where(here & (lane == v * 32 + u * SLOTS + s), part.astype(F32), head)
    head = head.astype(BF16)
    for s in range(SLOTS):
        tile = x_ref[:, s * BLK : (s + 1) * BLK]
        own_ref[s * BLK : (s + 1) * BLK, :] = tile
        for z in range(ZH):
            out_ref[z, s * BLK : (s + 1) * BLK, :] = tile
    for z in range(ZH):
        out_ref[z, TILES:, :] = head


def row_tiles(gij_ref, p, lane):
    li = jnp.full((1, 128), -1.0, F32)
    lk = jnp.full((1, 128), -1.0, F32)
    for z in range(ZL):
        here = (lane >> 5 == z) & ((lane & 31) < SLOTS_ROW)
        mine = jnp.broadcast_to(gij_ref[pl.ds(z * 32 + p, 1), :], (8, 128))
        li = jnp.where(here, (pltpu.roll(mine, z * 32, 1) if z else mine)[0:1], li)
        lk = jnp.where(here, pltpu.roll(mine, (64 + z * 32) % 128, 1)[0:1], lk)
    return li, lk


def left_kernel(
    g_ref, second_ref, zbuf_ref, gij_ref, adj_ref, dl_ref, rl_ref,
    ohi_ref, ohj_ref, list_ref, list_smem, sem,
):
    zh, y, zl, u, p, q = place()
    told = g_ref[...].astype(F32)
    for z in range(ZL):
        for h in range(ZH):
            gij_ref[z * 32 + h * Y : z * 32 + (h + 1) * Y, :] = told[:, z * HEAD + h, :]
        gij_ref[z * 32 + N_ROW : (z + 1) * 32, :] = jnp.zeros((32 - N_ROW, 128), F32)
    g = gij_ref[...]
    g = 16.0 * g + pltpu.roll(g, 96, 1)
    row128, lane128 = iota((128, 128), 0), iota((128, 128), 1)
    g = jnp.where(((row128 & 31) < N_ROW) & ((lane128 & 63) < SLOTS_ROW), g, -1.0)
    gij_ref[...] = g
    gt = g.T
    sub = iota((NB, 128), 0).astype(F32)
    wide = iota((128, NB), 1).astype(F32)
    for k in range(SLOTS_ROW):
        ohi_ref[:, k * 128 : (k + 1) * 128] = onehot(sub == gt[k : k + 1, :])
        ohj_ref[k * 128 : (k + 1) * 128, :] = onehot(wide == g[:, 64 + k : 65 + k])
    adj_b = dot(ohi_ref[...], ohj_ref[...]).astype(BF16)
    adj_ref[...] = adj_b
    lane = iota((1, 128), 1)
    rows, lanes = iota((32, 128), 0), iota((32, 128), 1)
    rows8, lanes8 = iota((8, 128), 0), iota((8, 128), 1)
    in_col = onehot(col_of(iota((32, NB), 1)) == iota((32, NB), 0))

    li, lk = row_tiles(gij_ref, p, lane)
    stack = jnp.where(row128 == 0, li, lk).T
    both = dot(onehot(wide == stack[:, 0:1]), adj_b) * dot(onehot(wide == stack[:, 1:2]), adj_b)
    count = lax.dot_general(in_col, both.astype(BF16), (((1,), (1,)), ((), ())), preferred_element_type=F32)
    owner = (lanes >> 5) * XC + (((lanes & 31) * 11) >> 5)
    wanted = (count > 0.5) & (owner != rows) & ((lanes & 31) < SLOTS_ROW)
    wanted = jnp.where(wanted, 1.0, 0.0)
    dl_ref[...] = wanted
    rl_ref[...] = dot(wanted.astype(BF16), onehot((row128 < lane128) & ((row128 >> 5) == (lane128 >> 5))))
    send_d = jnp.zeros((8, 128), F32)
    send_r = jnp.zeros((8, 128), F32)
    for z in range(ZL):
        send_d = jnp.where(rows8 == z, dl_ref[pl.ds(z * XC + u, 1), :], send_d)
        send_r = jnp.where(rows8 == z, rl_ref[pl.ds(z * XC + u, 1), :], send_r)
    zlist = jnp.zeros((8, 128), F32)
    for c in range(SLOTS):
        hit = (send_d > 0.5) & (send_r == float(c)) & ((lanes8 >> 5) == zl)
        code = jnp.sum(jnp.where(hit, ((lanes8 & 31) + 1).astype(F32), 0.0), axis=1, keepdims=True)
        zlist = jnp.where(lanes8 == c, code, zlist)

    list_ref[...] = zlist.astype(jnp.int32)
    copy = pltpu.make_async_copy(list_ref, list_smem, sem)
    copy.start()
    copy.wait()
    for d in range(ZL):
        for c in range(SLOTS):
            code = list_smem[d, c]

            @pl.when(code > 0)
            def _():
                k = code - 1
                src_u = (k * 11) >> 5
                start = pl.multiple_of(src_u * SECOND + (k - src_u * SLOTS) * BLK, 16)
                zbuf_ref[d, c * BLK : (c + 1) * BLK, :] = second_ref[pl.ds(start, BLK), :]


def term_kernel(
    blocks, gij_ref, adj_ref, dl_ref, rl_ref, list_ref, gt_ref, dy_ref, ry_ref,
):
    zh, y, zl, u, p, q = place()
    gt_ref[...] = gij_ref[...].T
    row128, lane128 = iota((128, 128), 0), iota((128, 128), 1)
    sub = iota((NB, 128), 0).astype(F32)
    adj_b = adj_ref[...]
    adj = adj_b.astype(F32)
    adj_t = adj.T
    mutual = adj * adj_t
    lane = iota((1, 128), 1)
    lanes = iota((32, 128), 1)
    rows = iota((32, 128), 0)
    in_row = onehot(row_of(iota((32, NB), 1)) == iota((32, NB), 0))
    in_col_t = onehot(col_of(iota((NB, 32), 0)) == iota((NB, 32), 1))

    ci = jnp.full((1, 128), -1.0, F32)
    cj = jnp.full((1, 128), -1.0, F32)
    for s in range(SLOTS):
        shift = (s * 32 + 128 - zl * 32) & 127
        here = (lane >> 5 == s) & ((lane & 31) < N_ROW)
        rows_i = jnp.broadcast_to(gt_ref[pl.ds(u * SLOTS + s, 1), :], (8, 128))
        rows_j = jnp.broadcast_to(gt_ref[pl.ds(64 + u * SLOTS + s, 1), :], (8, 128))
        ci = jnp.where(here, pltpu.roll(rows_i, shift, 1)[0:1], ci)
        cj = jnp.where(here, pltpu.roll(rows_j, shift, 1)[0:1], cj)
    of_i = onehot(sub == ci)
    both = dot(adj_b, onehot(sub == cj)) * dot(adj_b, of_i)
    pairs = jnp.broadcast_to(jnp.sum(mutual, axis=0, keepdims=True), (8, NB)).astype(BF16)
    plain = (ci == cj) & (ci >= 0.0) & (dot(pairs, of_i)[0:1] < 1.5)
    plain_f = jnp.where(plain, 1.0, 0.0)
    wanted = (dot(in_row, both.astype(BF16)) > 0.5) & ((lanes & 31) != rows) & (plain_f < 0.5)
    wanted = jnp.where(wanted, 1.0, 0.0)
    dy_ref[...] = wanted
    ry_ref[...] = dot(wanted.astype(BF16), onehot((row128 < lane128) & ((row128 & 7) == (lane128 & 7))))
    lanes8 = iota((8, 128), 1)
    rows8 = iota((8, 128), 0)
    plane_d = jnp.zeros((8, 128), F32)
    for z in range(ZH):
        plane = jnp.max(wanted[z * Y : (z + 1) * Y], axis=0, keepdims=True)
        plane_d = jnp.where(rows8 == z, plane, plane_d)
    plane_r = dot(plane_d.astype(BF16), onehot((row128 < lane128) & ((row128 & 31) == (lane128 & 31))))
    place_z = jnp.sum(jnp.where(rows8 == zh, plane_r, 0.0), axis=0, keepdims=True)
    place_z = place_z + (((lane & 31) >> 3) * ZROOM + 1).astype(F32)
    send_d = dy_ref[pl.ds(pl.multiple_of(zh * Y, 8), 8), :]
    send_r = ry_ref[pl.ds(pl.multiple_of(zh * Y, 8), 8), :]
    ylist = jnp.zeros((8, 128), F32)
    for c in range(ROOM):
        hit = (send_d > 0.5) & (send_r == float(c)) & ((lanes8 & 7) == y)
        code = jnp.sum(jnp.where(hit, place_z, 0.0), axis=1, keepdims=True)
        ylist = jnp.where(lanes8 == c, code, ylist)
    for c in range(ZROOM):
        hit = (plane_d > 0.5) & (plane_r == float(c)) & ((lanes8 & 31) == p)
        code = jnp.sum(jnp.where(hit, ((lanes8 >> 5) + 1).astype(F32), 0.0), axis=1, keepdims=True)
        ylist = jnp.where(lanes8 == 8 + c, code, ylist)

    li, lk = row_tiles(gij_ref, p, lane)

    right = jnp.where(ci >= 0.0, (lane + 1).astype(F32), 0.0)
    got_d, got_r = dy_ref[pl.ds(p, 1), :], ry_ref[pl.ds(p, 1), :]
    again = jnp.where(got_d > 0.5, ((lane & 7) * ROOM + 1).astype(F32) + got_r, 0.0)
    again = jnp.where(plain, float(PLAIN), again)
    again = jnp.where(((lane & 31) == p) & (ci >= 0.0), (OWN + (lane >> 5)).astype(F32), again)
    stack = jnp.where(row128 == 0, ci, jnp.where(row128 == 1, cj, jnp.where(row128 == 2, right, again))).T
    ci_c, cj_c = stack[:, 0:1], stack[:, 1:2]
    met_c = ci_c == lk
    linked = (jnp.where(met_c, stack[:, 2:3], 0.0), jnp.where(met_c, stack[:, 3:4], 0.0))
    meets = [jnp.zeros((8, 128), F32), jnp.zeros((8, 128), F32)]
    terms = jnp.zeros((8, 128), F32)
    for o in range(SLOTS):
        out_i, out_j = blocks[0, o].astype(F32), blocks[1, o].astype(F32)
        for n in range(2):
            met = jnp.sum(jnp.where(cj_c == out_j, linked[n], 0.0), axis=0, keepdims=True)
            meets[n] = jnp.where(rows8 == o, jnp.where(li == out_i, met, 0.0), meets[n])
        hit = plain & (ci == out_j) & ((lane & 31) != p)
        code = jnp.sum(jnp.where(hit, (lane + 1).astype(F32), 0.0), axis=1, keepdims=True)
        terms = jnp.where((rows8 == o) & (lanes8 == 64), code, terms)
    got_d, got_r = dl_ref[pl.ds(q, 1), :], rl_ref[pl.ds(q, 1), :]
    for t in range(LEFTS):
        if t < ZL * SLOTS:
            hit = (lane >> 5 == t // SLOTS) & (got_d > 0.5) & (got_r == float(t % SLOTS))
        else:
            hit = lane == zl * 32 + u * SLOTS + (t - ZL * SLOTS)
        for n in range(2):
            value = jnp.sum(jnp.where(hit, meets[n], 0.0), axis=1, keepdims=True)
            terms = jnp.where(lanes8 == n * 32 + t, value, terms)

    def per_dev(count):
        return dot(dot(in_row, (count * adj).astype(BF16)).astype(BF16), in_col_t)

    from_i, from_k = iota((NB, NB), 0), iota((NB, NB), 1)
    k_row = row_of(iota((1, NB), 1))
    k_col = col_of(iota((1, NB), 1))
    i_row = row_of(iota((NB, 1), 0))
    i_col = col_of(iota((NB, 1), 0))
    def fullest(total, parts, room):
        least = total
        for part in parts:
            least = jnp.minimum(least, jnp.maximum(part, total - part))
        return jnp.max(jnp.where(least > room + 0.5, 1.0, 0.0), keepdims=True)

    to_col = jnp.where(i_col != k_col, adj, 0.0).astype(BF16)
    total = per_dev(dot(adj_b, to_col))
    parts = [
        per_dev(dot(jnp.where(((k_col >> bit) & 1) == 1, adj, 0.0).astype(BF16), to_col)) for bit in (3, 4)
    ]
    over = fullest(total, parts, SLOTS)
    moving = jnp.where(i_row != k_row, adj, 0.0)
    single = jnp.sum(mutual, axis=1, keepdims=True) < 1.5
    target = jnp.where((from_i == from_k) & single, 0.0, adj).astype(BF16)
    total = per_dev(dot(moving.astype(BF16), target))
    parts = [
        per_dev(dot(jnp.where(((k_row >> bit) & 1) == 1, moving, 0.0).astype(BF16), target)) for bit in (0, 1, 2)
    ]
    over = jnp.maximum(over, fullest(total, parts, ROOM))
    asked = dot(jnp.where(i_row != k_row, adj_t, 0.0).astype(BF16), adj_b) * target.astype(F32)
    asked = dot(dot(in_row, onehot(asked > 0.5)).astype(BF16), in_col_t)
    over = jnp.maximum(over, fullest(asked, [], ZROOM))
    level = jnp.where((rows8 == 7) & (lanes8 == 0), over, 0.0)

    list_ref[0:ZLIST, :] = ylist.astype(jnp.int32)
    list_ref[ZLIST:TERMS, :] = level.astype(jnp.int32)
    list_ref[TERMS:, :] = terms.astype(jnp.int32)


def tile_at(start):
    return pl.ds(pl.multiple_of(start, 16), BLK)


def left_at(t, left_ref, own_ref):
    if t < ZL * SLOTS:
        return left_ref.at[t * BLK : (t + 1) * BLK, :]
    t -= ZL * SLOTS
    return own_ref.at[t * BLK : (t + 1) * BLK, :]


def panel_start(code):
    r = code - 1
    return ((r & 7) * ZH + ((r >> 3) & 3)) * PANEL + (r >> 5) * BLK


def square_kernel(lists, own_ref, left_ref, right_ref, out_ref, near_ref, acc_ref):
    for o in range(SLOTS):
        part = slice(o * BLK, (o + 1) * BLK)
        acc_ref[...] = jnp.zeros((BLK, BLK), F32)
        for t in range(LEFTS):
            code = lists[TERMS + o, t]
            left = left_at(t, left_ref, own_ref)

            @pl.when(code > 0)
            def _():
                acc_ref[...] += dot(left[...], right_ref[tile_at(panel_start(code)), :])

        tile = acc_ref[...].astype(BF16)
        near_ref[part, :] = tile
        code = lists[TERMS + o, 64]

        @pl.when(code > 0)
        def _():
            tile = right_ref[tile_at(panel_start(code)), :]
            near_ref[TILES + o * BLK : TILES + (o + 1) * BLK, :] = dot(tile, tile).astype(BF16)

    for z in range(ZH):
        for c in range(ZROOM):
            code = lists[z, 8 + c]

            @pl.when((code > 0) & (code <= SLOTS))
            def _():
                out_ref[z, c * BLK : (c + 1) * BLK, :] = near_ref[tile_at((code - 1) * BLK), :]


def send_kernel(lists, square_ref, send_ref):
    for d in range(Y):
        for c in range(ROOM):
            code = lists[d, c]

            @pl.when((code > 0) & (code <= ZH * ZROOM))
            def _():
                send_ref[d, c * BLK : (c + 1) * BLK, :] = square_ref[tile_at((code - 1) * BLK), :]


def cube_kernel(lists, blocks, own_ref, left_ref, near_ref, right_ref, out_ref, level_ref, acc_ref):
    for o in range(SLOTS):
        part = slice(o * BLK, (o + 1) * BLK)
        acc_ref[...] = jnp.zeros((BLK, BLK), F32)
        for t in range(LEFTS):
            code = lists[TERMS + o, 32 + t]
            left = left_at(t, left_ref, own_ref)

            @pl.when((code > 0) & (code <= Y * ROOM))
            def _():
                acc_ref[...] += dot(left[...], right_ref[tile_at((code - 1) * BLK), :])

            @pl.when(code >= OWN)
            def _():
                start = jnp.where(code == PLAIN, TILES + o * BLK, (code - OWN) * BLK)
                acc_ref[...] += dot(left[...], near_ref[tile_at(start), :])

        value = 1.5 * own_ref[part, :].astype(F32) - 0.5 * acc_ref[...]
        out_ref[:, part] = jnp.where(blocks[0, o] >= 0, value, 0.0).astype(BF16)
    level_ref[0] = lists[TERMS - 1, 0]


def swap(value, axes):
    return lax.all_to_all(value, axes, 0, 0, tiled=True)


def like(*shape, dtype=BF16):
    return jax.ShapeDtypeStruct(shape, dtype)


def per_device(x, blocks):
    first, own = pl.pallas_call(
        pack_kernel,
        out_shape=(like(ZH, PANEL, BLK), like(TILES, BLK)),
        in_specs=[SMEM, VMEM], out_specs=(VMEM, VMEM), compiler_params=PARAMS, name="pack",
    )(blocks, x)
    first = swap(first, "zh")
    right = lax.all_gather(first.reshape(ZH * PANEL, BLK), "y", axis=0, tiled=True)
    heads = first[:, TILES:].reshape(ZH * HEAD, 128)
    second = lax.all_gather(jnp.concatenate([own, heads], axis=0), ("x", "c"), axis=0)
    heads = jnp.sum(second[:, TILES:].reshape(XC * ZH, HEAD, 128).astype(F32), axis=0).astype(BF16)
    heads = jnp.broadcast_to(heads[None], (Y * ZL, HEAD, 128)).reshape(Y * ZL * HEAD, 128)
    heads = swap(heads, ("y", "zl")).reshape(Y, ZL * HEAD, 128)
    zbuf, known, adjacent, wanted, ranks = pl.pallas_call(
        left_kernel,
        out_shape=(
            like(ZL, TILES, BLK), like(128, 128, dtype=F32), like(NB, NB),
            like(32, 128, dtype=F32), like(32, 128, dtype=F32),
        ),
        in_specs=[VMEM, VMEM], out_specs=(VMEM,) * 5,
        scratch_shapes=[
            pltpu.VMEM((NB, SLOTS_ROW * 128), BF16), pltpu.VMEM((SLOTS_ROW * 128, NB), BF16),
            pltpu.VMEM((8, 128), jnp.int32), pltpu.SMEM((8, 128), jnp.int32), pltpu.SemaphoreType.DMA,
        ],
        compiler_params=PARAMS, name="left",
    )(heads, second.reshape(XC * SECOND, BLK))
    left = swap(zbuf, "zl").reshape(ZL * TILES, BLK)
    lists = pl.pallas_call(
        term_kernel,
        out_shape=like(TERMS + 8, 128, dtype=jnp.int32),
        in_specs=[SMEM] + [VMEM] * 4, out_specs=VMEM,
        scratch_shapes=[pltpu.VMEM((128, 128), F32), pltpu.VMEM((32, 128), F32), pltpu.VMEM((32, 128), F32)],
        cost_estimate=pl.CostEstimate(flops=2_000_000_000, bytes_accessed=1_000_000, transcendentals=0),
        compiler_params=PARAMS, name="term",
    )(blocks, known, adjacent, wanted, ranks)
    square, near = pl.pallas_call(
        square_kernel,
        out_shape=(like(ZH, ZROOM * BLK, BLK), like(2 * TILES, BLK)),
        in_specs=[SMEM] + [VMEM] * 3, out_specs=(VMEM, VMEM),
        scratch_shapes=[pltpu.VMEM((BLK, BLK), F32)], compiler_params=PARAMS, name="square",
    )(lists, own, left, right)
    square = swap(square, "zh").reshape(ZH * ZROOM * BLK, BLK)
    send = pl.pallas_call(
        send_kernel,
        out_shape=like(Y, ROOM * BLK, BLK),
        in_specs=[SMEM, VMEM], out_specs=VMEM, compiler_params=PARAMS, name="send",
    )(lists, square)
    result, level = pl.pallas_call(
        cube_kernel,
        out_shape=(like(*x.shape), like(1, dtype=jnp.int32)),
        in_specs=[SMEM, SMEM] + [VMEM] * 4, out_specs=(VMEM, SMEM),
        scratch_shapes=[pltpu.VMEM((BLK, BLK), F32)], compiler_params=PARAMS, name="cube",
    )(lists, blocks, own, left, near, swap(send, "y").reshape(Y * ROOM * BLK, BLK))
    result, level, x, blocks = lax.optimization_barrier((result, level, x, blocks))
    return lax.cond(level[0] > 0, lambda: general(x, blocks), lambda: result)


def solution(mesh):
    fine = Mesh(mesh.devices.reshape(ZH, Y, ZL, X, C), ROW + COL)
    return jax.shard_map(
        per_device,
        mesh=fine,
        in_specs=(P(ROW, COL), P(ROW, COL)),
        out_specs=P(ROW, COL),
        check_vma=False,
    )
```
